32 devices in a mesh: dp: 2 (over x), seq: 16 (over z, y, core).
Axes of the slice: x: 2, y: 2, z: 4, core: 2. Of those that a mesh axis runs over, the one named last changes fastest.
Arguments:
- queries: bfloat16 [4096, 2048], P(('dp', 'seq')), may hold values from -8 to 8
- keys: bfloat16 [4096, 1024], P(('dp', 'seq')), may hold values from -15 to 15
- values: bfloat16 [4096, 1024], P(('dp', 'seq')), may hold values from -6 to 6
- output_gradient: bfloat16 [4096, 2048], P(('dp', 'seq')), may hold values from -6 to 6
- doc_lengths: int32 [32], replicated, may hold values from 1 to 512, 4096 in all
Outputs:
- attended: bfloat16 [4096, 2048], P(('dp', 'seq'))
- q_grad: float32 [4096, 2048], P(('dp', 'seq'))
- k_grad: float32 [4096, 1024], P(('dp', 'seq'))
- v_grad: float32 [4096, 1024], P(('dp', 'seq'))
The draws below stay inside these ranges and needn't reach their ends.
Inputs may be any that keep to these rules, and one draw needn't show every extreme that they name: `doc_lengths`: the documents fill all 4096 positions of the sequence in order, and the longest has exactly 512 tokens.
All inputs are finite; a program needn't handle non-finite values.
Results may differ from the reference program's by a relative error of at most 0.04.
Values may be sent and summed in bfloat16 or wider, within the bound.
No kernel may reach another device: no remote copies, remote signals or barrier semaphores. Data moves between devices by JAX's collectives and lax.ppermute only.
A program may use at most 64 MiB of HBM per device.

```python
import math
import jax
import jax.numpy as jnp
import numpy as np
from jax import lax

QUERY_HEADS = 16
KEY_VALUE_HEADS = 8
HEAD_SIZE = 128
LOCAL_WINDOW = 256
PACKED_TOKENS = 4096
DOCS = 32
MOST = 512


def draw_queries(key, part):
    noise_seed, scale_seed = jax.random.split(jax.random.fold_in(key, 3))
    base_offset = jax.random.truncated_normal(noise_seed, -3.0, 3.0, (PACKED_TOKENS, QUERY_HEADS, HEAD_SIZE), jnp.float32)
    scale_values = jnp.exp(jax.random.uniform(scale_seed, (PACKED_TOKENS, QUERY_HEADS, 1), jnp.float32, jnp.log(0.5), jnp.log(2.0)))
    final_result = base_offset * scale_values
    return final_result.reshape(PACKED_TOKENS, QUERY_HEADS * HEAD_SIZE).astype(jnp.bfloat16)


def draw_keys(key, part):
    noise_seed, scale_seed = jax.random.split(jax.random.fold_in(key, 5))
    base_offset = jax.random.truncated_normal(noise_seed, -3.0, 3.0, (PACKED_TOKENS, KEY_VALUE_HEADS, HEAD_SIZE), jnp.float32)
    scale_values = jnp.exp(jax.random.uniform(scale_seed, (PACKED_TOKENS, KEY_VALUE_HEADS, 1), jnp.float32, jnp.log(0.5), jnp.log(5.0)))
    final_result = base_offset * scale_values
    return final_result.reshape(PACKED_TOKENS, KEY_VALUE_HEADS * HEAD_SIZE).astype(jnp.bfloat16)


def block_scale(stream_key, extent, pieces, least, largest):
    factor_of, own = 1.0, jax.random.fold_in(stream_key, 6)
    for dim, blocks in pieces:
        heights = jnp.exp(jax.random.uniform(jax.random.fold_in(own, dim), (blocks,), jnp.float32, least / len(pieces), largest / len(pieces)))
        factor_of = factor_of * jnp.repeat(heights, extent[dim] // blocks).reshape([-1 if axis == dim else 1 for axis in range(len(extent))])
    return factor_of


def profile(amount, total, limit, skew):
    loads = [(1 << 20) // math.isqrt(grade ** skew) + 1 for grade in range(2, amount + 1)]
    surplus, given = total - limit - (amount - 1), [1] * (amount - 1)
    while surplus > 0:
        movable = [i for i in range(amount - 1) if given[i] < limit]
        mass, budget = sum([loads[i] for i in movable]), surplus
        for i in movable:
            extra = min(limit - given[i], max(1, budget * loads[i] // mass), surplus)
            given[i] = given[i] + extra
            surplus = surplus - extra
    return np.array([limit] + given)


def uneven_parts(own_key, number_of, total, bound, slope):
    if number_of == 2:
        one = jax.random.randint(own_key, (), max(1, total - bound), min(bound, total - 1) + 1)
        return jnp.stack([one, total - one])
    tallies = jnp.asarray(profile(number_of, total, bound, slope), jnp.int32)
    couples = (number_of - 1) // 2
    source_of, taker = tallies[1:1 + 2 * couples:2], tallies[2:2 + 2 * couples:2]
    room = jnp.minimum(source_of - 1, bound - taker)
    moved = jax.random.randint(jax.random.fold_in(own_key, 1), (couples,), 0, 1 << 20) % (room + 1)
    tallies = tallies.at[1:1 + 2 * couples:2].set(source_of - moved).at[2:2 + 2 * couples:2].set(taker + moved)
    return tallies[jax.random.permutation(jax.random.fold_in(own_key, 2), number_of)]


def bell_draw(rng, shape, deviation, most, shards=(), held_as=jnp.bfloat16):
    loudness = block_scale(rng, shape, shards, -0.22, 0.18) if shards else 1.0
    values = jax.random.normal(rng, shape, jnp.float32) * deviation * loudness
    return jnp.minimum(jnp.maximum(values, -most), most).astype(held_as)


def setup_inputs(seed: int = 0) -> dict:
    streams_of = jax.random.split(jax.random.key(seed), 6)
    return {
        "queries": draw_queries(jax.random.fold_in(streams_of[5], 71), 0),
        "keys": draw_keys(jax.random.fold_in(streams_of[5], 71), 0),
        "values": bell_draw(streams_of[2], (PACKED_TOKENS, KEY_VALUE_HEADS * HEAD_SIZE), 1.0, 6.0, ((0, 32),)),
        "output_gradient": bell_draw(streams_of[3], (PACKED_TOKENS, QUERY_HEADS * HEAD_SIZE), 1.0, 6.0, ((0, 32),)),
        "doc_lengths": uneven_parts(streams_of[4], DOCS, PACKED_TOKENS, MOST, 2).astype(jnp.int32),
    }


score_scale = 168.0 ** -0.5


def doc_index(positions, doc_ends):
    doc_count = jnp.sum((doc_ends[None, :] <= positions[:, None]).astype(jnp.int32), axis=1)
    return jnp.where(positions < 0, -1, doc_count).astype(jnp.int32)


def live_pairs(query_pos, key_pos, doc_ends):
    spacing = query_pos[:, None] - key_pos[None, :]
    same_doc = doc_index(query_pos, doc_ends)[:, None] == doc_index(key_pos, doc_ends)[None, :]
    return same_doc & (spacing >= 0) & (spacing < LOCAL_WINDOW)


def reference(queries, keys, values, output_gradient, doc_lengths):
    query_groups = QUERY_HEADS // KEY_VALUE_HEADS
    rows_per_block = 256
    span_length = rows_per_block + LOCAL_WINDOW
    doc_ends = jnp.cumsum(doc_lengths).astype(jnp.int32)
    padding_amount = jnp.zeros((LOCAL_WINDOW, KEY_VALUE_HEADS * HEAD_SIZE), keys.dtype)
    key_padding = jnp.concatenate([padding_amount, keys], axis=0)
    value_padding = jnp.concatenate([padding_amount, values], axis=0)

    def one_block(number, carry):
        attended, q_grad, padded_keys, padded_values = carry
        start_index = (number * rows_per_block).astype(jnp.int32)
        heads_of_queries = lax.dynamic_slice_in_dim(queries, start_index, rows_per_block, 0).astype(jnp.float32).reshape(rows_per_block, KEY_VALUE_HEADS, query_groups, HEAD_SIZE)
        head_gradients = lax.dynamic_slice_in_dim(output_gradient, start_index, rows_per_block, 0).astype(jnp.float32).reshape(rows_per_block, KEY_VALUE_HEADS, query_groups, HEAD_SIZE)
        heads_of_keys = lax.dynamic_slice_in_dim(key_padding, start_index, span_length, 0).astype(jnp.float32).reshape(span_length, KEY_VALUE_HEADS, HEAD_SIZE)
        heads_of_values = lax.dynamic_slice_in_dim(value_padding, start_index, span_length, 0).astype(jnp.float32).reshape(span_length, KEY_VALUE_HEADS, HEAD_SIZE)
        query_pos = start_index + jnp.arange(rows_per_block, dtype=jnp.int32)
        key_pos = start_index - LOCAL_WINDOW + jnp.arange(span_length, dtype=jnp.int32)
        live_mask = live_pairs(query_pos, key_pos, doc_ends)
        scores = jnp.einsum("qgrd,kgd->grqk", heads_of_queries, heads_of_keys) * score_scale
        scores = jnp.where(live_mask[None, None], scores, -jnp.inf)
        row_max = jnp.max(scores, axis=-1)
        row_total = jnp.sum(jnp.exp(scores - row_max[..., None]), axis=-1)
        log_total = row_max + jnp.log(row_total)
        probs_full = jnp.exp(scores - log_total[..., None])
        weights = lax.optimization_barrier(probs_full.astype(jnp.bfloat16)).astype(jnp.float32)
        context_rows = jnp.einsum("grqk,kgd->qgrd", weights, heads_of_values).astype(jnp.bfloat16)
        context_wide = context_rows.astype(jnp.float32)
        grad_dot = jnp.transpose(jnp.sum(head_gradients * context_wide, axis=-1), (1, 2, 0))
        prob_grad = jnp.einsum("qgrd,kgd->grqk", head_gradients, heads_of_values)
        score_grad = (probs_full * (prob_grad - grad_dot[..., None]) * score_scale).astype(jnp.bfloat16)
        score_grad = lax.optimization_barrier(score_grad).astype(jnp.float32)
        query_part = jnp.einsum("grqk,kgd->qgrd", score_grad, heads_of_keys)
        key_portion = jnp.einsum("grqk,qgrd->kgd", score_grad, heads_of_queries)
        value_portion = jnp.einsum("grqk,qgrd->kgd", weights, head_gradients)
        attended = lax.dynamic_update_slice_in_dim(attended, context_rows.reshape(rows_per_block, QUERY_HEADS * HEAD_SIZE), start_index, 0)
        q_grad = lax.dynamic_update_slice_in_dim(q_grad, query_part.reshape(rows_per_block, QUERY_HEADS * HEAD_SIZE), start_index, 0)
        prior_keys = lax.dynamic_slice_in_dim(padded_keys, start_index, span_length, 0)
        padded_keys = lax.dynamic_update_slice_in_dim(padded_keys, prior_keys + key_portion.reshape(span_length, KEY_VALUE_HEADS * HEAD_SIZE), start_index, 0)
        prior_values = lax.dynamic_slice_in_dim(padded_values, start_index, span_length, 0)
        padded_values = lax.dynamic_update_slice_in_dim(padded_values, prior_values + value_portion.reshape(span_length, KEY_VALUE_HEADS * HEAD_SIZE), start_index, 0)
        return attended, q_grad, padded_keys, padded_values

    initial = (jnp.zeros((PACKED_TOKENS, QUERY_HEADS * HEAD_SIZE), jnp.bfloat16), jnp.zeros((PACKED_TOKENS, QUERY_HEADS * HEAD_SIZE), jnp.float32),
               jnp.zeros((PACKED_TOKENS + LOCAL_WINDOW, KEY_VALUE_HEADS * HEAD_SIZE), jnp.float32), jnp.zeros((PACKED_TOKENS + LOCAL_WINDOW, KEY_VALUE_HEADS * HEAD_SIZE), jnp.float32))
    attended, q_grad, padded_keys, padded_values = lax.fori_loop(0, PACKED_TOKENS // rows_per_block, one_block, initial)
    return attended, q_grad, padded_keys[LOCAL_WINDOW:], padded_values[LOCAL_WINDOW:]
```

```python
import functools

import jax
import jax.numpy as jnp
from jax import lax
from jax.experimental import pallas as pl
from jax.experimental.pallas import tpu as pltpu
from jax.sharding import PartitionSpec as P

QUERY_HEADS = 16
KEY_VALUE_HEADS = 8
HEAD_SIZE = 128
LOCAL_WINDOW = 256
GROUP = QUERY_HEADS // KEY_VALUE_HEADS
AXES = ("dp", "seq")

score_scale = 168.0 ** (-0.5)
LOG2E = 1.4426950408889634
NEGATIVE = -1e30
STEP_HEADS = 2

CONTRACT_LAST = (((1,), (1,)), ((), ()))
CONTRACT_FIRST = (((0,), (0,)), ((), ()))


def dot(a, b):
    return jnp.dot(a, b, preferred_element_type=jnp.float32)


def dot_last(a, b):
    return lax.dot_general(a, b, CONTRACT_LAST, preferred_element_type=jnp.float32)


def dot_first(a, b):
    return lax.dot_general(a, b, CONTRACT_FIRST, preferred_element_type=jnp.float32)


def stacked(ref, head):
    wide = GROUP * HEAD_SIZE
    return jnp.concatenate(
        [ref[:, head * wide + j * HEAD_SIZE : head * wide + (j + 1) * HEAD_SIZE] for j in range(GROUP)],
        axis=0,
    )


def columns(ref, head):
    return ref[:, head * HEAD_SIZE : (head + 1) * HEAD_SIZE]


def fill_bias(rank_ref, lens_ref, bias_ref, rows):
    docs = lens_ref.shape[1]
    first = rank_ref[0] * rows
    later = lax.broadcasted_iota(jnp.int32, (docs, docs), 0)
    earlier = lax.broadcasted_iota(jnp.int32, (docs, docs), 1)
    lens = jnp.broadcast_to(lens_ref[...].astype(jnp.float32), (docs, docs))
    ends = jnp.sum(jnp.where(earlier <= later, lens, 0.0), axis=1, keepdims=True)
    wide = GROUP * rows
    query = first + lax.broadcasted_iota(jnp.int32, (1, wide), 1) % rows
    ended = jnp.where(ends <= query.astype(jnp.float32), ends, 0.0)
    start = jnp.max(ended, axis=0, keepdims=True).astype(jnp.int32)
    lowest = jnp.maximum(start, query - (LOCAL_WINDOW - 1))
    key = first - 2 * rows + lax.broadcasted_iota(jnp.int32, (3 * rows, wide), 0)
    bias_ref[...] = jnp.where((key >= lowest) & (key <= query), 0.0, NEGATIVE)


def value_kernel(
    rank_ref, lens_ref, q_ref, g_ref, k2_ref, ka_ref, kb_ref, k0_ref,
    prob_ref, dv2_ref, dv1_ref, dv0_ref, bias_ref,
):
    rows = q_ref.shape[0]

    @pl.when(pl.program_id(0) == 0)
    def _():
        fill_bias(rank_ref, lens_ref, bias_ref, rows)

    for head in range(STEP_HEADS):
        queries = stacked(q_ref, head)
        keys = jnp.concatenate(
            [columns(k2_ref, head), columns(ka_ref, head) + columns(kb_ref, head), columns(k0_ref, head)],
            axis=0,
        )
        scores = dot_last(keys, queries) * (score_scale * LOG2E) + bias_ref[...]
        top = jnp.max(scores, axis=0, keepdims=True)
        raised = jnp.exp2(scores - top)
        total = jnp.sum(raised, axis=0, keepdims=True)
        prob = (raised * (1.0 / total)).astype(jnp.bfloat16)
        prob_ref[head] = prob
        grads = dot(prob, stacked(g_ref, head))
        here = slice(head * HEAD_SIZE, (head + 1) * HEAD_SIZE)
        dv2_ref[:, here] = grads[:rows].astype(jnp.bfloat16)
        dv1_ref[:, here] = grads[rows : 2 * rows].astype(jnp.bfloat16)
        dv0_ref[:, here] = grads[2 * rows :]


def key_kernel(
    prob_ref, q_ref, g_ref, v2_ref, va_ref, vb_ref, v0_ref,
    dscore_ref, dk2_ref, dk1_ref, dk0_ref,
):
    rows = q_ref.shape[0]
    for head in range(STEP_HEADS):
        values = jnp.concatenate(
            [columns(v2_ref, head), columns(va_ref, head) + columns(vb_ref, head), columns(v0_ref, head)],
            axis=0,
        )
        dprob = dot_last(values, stacked(g_ref, head))
        prob = prob_ref[head].astype(jnp.float32)
        delta = jnp.sum(prob * dprob, axis=0, keepdims=True)
        dscore = (prob * (dprob - delta) * score_scale).astype(jnp.bfloat16)
        dscore_ref[head] = dscore
        grads = dot(dscore, stacked(q_ref, head))
        here = slice(head * HEAD_SIZE, (head + 1) * HEAD_SIZE)
        dk2_ref[:, here] = grads[:rows].astype(jnp.bfloat16)
        dk1_ref[:, here] = grads[rows : 2 * rows].astype(jnp.bfloat16)
        dk0_ref[:, here] = grads[2 * rows :]


def query_kernel(
    prob_ref, dscore_ref, k2_ref, ka_ref, kb_ref, k0_ref, v2_ref, va_ref, vb_ref, v0_ref,
    out_ref, dq_ref,
):
    rows = out_ref.shape[0]
    for head in range(STEP_HEADS):
        values = jnp.concatenate(
            [columns(v2_ref, head), columns(va_ref, head) + columns(vb_ref, head), columns(v0_ref, head)],
            axis=0,
        )
        keys = jnp.concatenate(
            [columns(k2_ref, head), columns(ka_ref, head) + columns(kb_ref, head), columns(k0_ref, head)],
            axis=0,
        )
        out = dot_first(prob_ref[head], values)
        grads = dot_first(dscore_ref[head], keys)
        for j in range(GROUP):
            at = (head * GROUP + j) * HEAD_SIZE
            out_ref[:, at : at + HEAD_SIZE] = out[j * rows : (j + 1) * rows].astype(jnp.bfloat16)
            dq_ref[:, at : at + HEAD_SIZE] = grads[j * rows : (j + 1) * rows]


def shape(dims, dtype):
    return jax.ShapeDtypeStruct(dims, dtype)


def on_device(queries, keys, values, output_gradient, doc_lengths):
    rows = queries.shape[0]
    devices = lax.axis_size(AXES)
    rank = lax.axis_index(AXES)
    odd = rank % 2 == 1
    docs = doc_lengths.shape[0]

    ahead = [(r, r + 2) for r in range(devices - 2)]
    behind = [(r + 2, r) for r in range(devices - 2)]
    to_odd = [(r, r + 1) for r in range(0, devices, 2)]
    to_even = [(r + 1, r) for r in range(0, devices, 2)]
    swap = to_odd + to_even

    narrow = STEP_HEADS * HEAD_SIZE
    steps = KEY_VALUE_HEADS // STEP_HEADS
    wide_block = pl.BlockSpec((rows, GROUP * narrow), lambda i: (0, i))
    block = pl.BlockSpec((rows, narrow), lambda i: (0, i))
    pair_block = pl.BlockSpec((STEP_HEADS, 3 * rows, GROUP * rows), lambda i: (i, 0, 0))
    kv_width = keys.shape[1]
    pairs = shape((KEY_VALUE_HEADS, 3 * rows, GROUP * rows), jnp.bfloat16)
    half = shape((rows, kv_width), jnp.bfloat16)
    full = shape((rows, kv_width), jnp.float32)

    k2 = lax.ppermute(keys, AXES, ahead)
    v2 = lax.ppermute(values, AXES, ahead)
    ka = lax.ppermute(keys, AXES, to_odd)
    va = lax.ppermute(values, AXES, to_odd)
    kb = lax.ppermute(k2, AXES, to_even)
    vb = lax.ppermute(v2, AXES, to_even)

    prob, dv2, dv1, dv0 = pl.pallas_call(
        value_kernel,
        grid=(steps,),
        in_specs=[
            pl.BlockSpec(memory_space=pltpu.SMEM),
            pl.BlockSpec((1, docs), lambda i: (0, 0)),
            wide_block, wide_block, block, block, block, block,
        ],
        out_specs=[pair_block, block, block, block],
        out_shape=[pairs, half, half, full],
        scratch_shapes=[pltpu.VMEM((3 * rows, GROUP * rows), jnp.float32)],
        name="value_grads",
    )(rank.reshape(1), doc_lengths.reshape(1, docs), queries, output_gradient, k2, ka, kb, keys)
    dv1 = lax.ppermute(dv1, AXES, swap).astype(jnp.float32)
    dv_send = (dv2.astype(jnp.float32) + jnp.where(odd, dv1, 0.0)).astype(jnp.bfloat16)
    dv_back = lax.ppermute(dv_send, AXES, behind)

    dscore, dk2, dk1, dk0 = pl.pallas_call(
        key_kernel,
        grid=(steps,),
        in_specs=[pair_block, wide_block, wide_block, block, block, block, block],
        out_specs=[pair_block, block, block, block],
        out_shape=[pairs, half, half, full],
        name="key_grads",
    )(prob, queries, output_gradient, v2, va, vb, values)
    dk1 = lax.ppermute(dk1, AXES, swap).astype(jnp.float32)
    dk_send = (dk2.astype(jnp.float32) + jnp.where(odd, dk1, 0.0)).astype(jnp.bfloat16)
    dk_back = lax.ppermute(dk_send, AXES, behind)

    attended, dq = pl.pallas_call(
        query_kernel,
        grid=(steps,),
        in_specs=[pair_block, pair_block] + [block] * 8,
        out_specs=[wide_block, wide_block],
        out_shape=[shape(queries.shape, jnp.bfloat16), shape(queries.shape, jnp.float32)],
        name="query_grads",
    )(prob, dscore, k2, ka, kb, keys, v2, va, vb, values)

    dv = dv0 + jnp.where(odd, 0.0, dv1) + dv_back.astype(jnp.float32)
    dk = dk0 + jnp.where(odd, 0.0, dk1) + dk_back.astype(jnp.float32)
    return attended, dq, dk, dv


def solution(mesh):
    split = P(AXES, None)
    return jax.shard_map(
        on_device,
        mesh=mesh,
        in_specs=(split, split, split, split, P()),
        out_specs=(split, split, split, split),
        check_vma=False,
    )
```

```python
import jax
import jax.numpy as jnp
from jax import lax
from jax.experimental import pallas as pl
from jax.experimental.pallas import tpu as pltpu
from jax.sharding import PartitionSpec as P

QUERY_HEADS = 16
KEY_VALUE_HEADS = 8
HEAD_SIZE = 128
LOCAL_WINDOW = 256
GROUP = QUERY_HEADS // KEY_VALUE_HEADS
CORES = 2
CORE_HEADS = KEY_VALUE_HEADS // CORES
AXES = ("dp", "seq")

score_scale = 168.0 ** (-0.5)
LOG2E = 1.4426950408889634
NEGATIVE = -1e30

CONTRACT_LAST = (((1,), (1,)), ((), ()))
CONTRACT_FIRST = (((0,), (0,)), ((), ()))


def dot(a, b):
    return jnp.dot(a, b, preferred_element_type=jnp.float32)


def dot_last(a, b):
    return lax.dot_general(a, b, CONTRACT_LAST, preferred_element_type=jnp.float32)


def dot_first(a, b):
    return lax.dot_general(a, b, CONTRACT_FIRST, preferred_element_type=jnp.float32)


def span(head):
    return slice(head * HEAD_SIZE, (head + 1) * HEAD_SIZE)


def both(odd, mine, other, head):
    a, b = mine[:, span(head)], other[:, span(head)]
    return jnp.where(odd, b, a), jnp.where(odd, a, b)


def stacked(odd, mine, other, head):
    pieces = [both(odd, mine, other, head * GROUP + j) for j in range(GROUP)]
    return [jnp.concatenate([piece[block] for piece in pieces], axis=0) for block in range(CORES)]


def put(odd, mine, other, head, first, second):
    mine[:, span(head)] = jnp.where(odd, second, first).astype(mine.dtype)
    other[:, span(head)] = jnp.where(odd, first, second).astype(other.dtype)


def split_kernel(rank_ref, *refs):
    count = len(refs) // 3
    odd = rank_ref[0] % 2
    for i in range(count):
        source, mine, other = refs[i], refs[count + 2 * i], refs[count + 2 * i + 1]
        width = source.shape[1] // 2

        @pl.when(odd == 0)
        def _():
            mine[...] = source[:, :width]
            other[...] = source[:, width:]

        @pl.when(odd == 1)
        def _():
            mine[...] = source[:, width:]
            other[...] = source[:, :width]


def bias_kernel(rank_ref, lens_ref, bias_ref):
    _, span_rows, rows = bias_ref.shape
    docs = lens_ref.shape[1]
    later = lax.broadcasted_iota(jnp.int32, (docs, docs), 0)
    earlier = lax.broadcasted_iota(jnp.int32, (docs, docs), 1)
    lens = jnp.broadcast_to(lens_ref[...].astype(jnp.float32), (docs, docs))
    ends = jnp.sum(jnp.where(earlier <= later, lens, 0.0), axis=1, keepdims=True)
    for block in range(CORES):
        first = (rank_ref[0] // CORES * CORES + block) * rows
        query = first + lax.broadcasted_iota(jnp.int32, (1, rows), 1)
        ended = jnp.where(ends <= query.astype(jnp.float32), ends, 0.0)
        start = jnp.max(ended, axis=0, keepdims=True).astype(jnp.int32)
        lowest = jnp.maximum(start, query - (LOCAL_WINDOW - 1))
        key = first - 2 * rows + lax.broadcasted_iota(jnp.int32, (span_rows, rows), 0)
        bias_ref[block] = jnp.where((key >= lowest) & (key <= query), 0.0, NEGATIVE)


def value_kernel(
    rank_ref, bias_ref, qm, qo, gm, go, km, ko, k2m, k2o,
    prob_ref, dvm, dvo,
):
    rows = qm.shape[0]
    odd = rank_ref[0] % 2 == 1
    for head in range(CORE_HEADS):
        blocks = both(odd, k2m, k2o, head) + both(odd, km, ko, head)
        queries = stacked(odd, qm, qo, head)
        gradients = stacked(odd, gm, go, head)
        grads = []
        for block in range(CORES):
            keys = jnp.concatenate(blocks[block : block + 3], axis=0)
            bias = jnp.concatenate([bias_ref[block]] * GROUP, axis=1)
            scores = dot_last(keys, queries[block]) * (score_scale * LOG2E) + bias
            top = jnp.max(scores, axis=0, keepdims=True)
            raised = jnp.exp2(scores - top)
            total = jnp.sum(raised, axis=0, keepdims=True)
            prob = (raised * (1.0 / total)).astype(jnp.bfloat16)
            prob_ref[head * CORES + block] = prob
            grads.append(dot(prob[: (2 - block) * rows], gradients[block]))
        put(odd, dvm, dvo, head, grads[0][:rows], grads[0][rows:] + grads[1])


def key_kernel(
    rank_ref, prob_ref, qm, qo, gm, go, vm, vo, v2m, v2o,
    dscore_ref, dkm, dko,
):
    rows = qm.shape[0]
    odd = rank_ref[0] % 2 == 1
    for head in range(CORE_HEADS):
        blocks = both(odd, v2m, v2o, head) + both(odd, vm, vo, head)
        queries = stacked(odd, qm, qo, head)
        gradients = stacked(odd, gm, go, head)
        grads = []
        for block in range(CORES):
            values = jnp.concatenate(blocks[block : block + 3], axis=0)
            dprob = dot_last(values, gradients[block])
            prob = prob_ref[head * CORES + block].astype(jnp.float32)
            delta = jnp.sum(prob * dprob, axis=0, keepdims=True)
            dscore = (prob * ((dprob - delta) * score_scale)).astype(jnp.bfloat16)
            dscore_ref[head * CORES + block] = dscore
            grads.append(dot(dscore[: (2 - block) * rows], queries[block]))
        put(odd, dkm, dko, head, grads[0][:rows], grads[0][rows:] + grads[1])


def rest_kernel(
    rank_ref, prob_ref, dscore_ref, qm, qo, gm, go, km, ko, k2m, k2o, vm, vo, v2m, v2o,
    outm, outo, dqm, dqo, dkm, dko, dvm, dvo,
):
    rows = qm.shape[0]
    odd = rank_ref[0] % 2 == 1
    for head in range(CORE_HEADS):
        keys = both(odd, k2m, k2o, head) + both(odd, km, ko, head)
        values = both(odd, v2m, v2o, head) + both(odd, vm, vo, head)
        queries = stacked(odd, qm, qo, head)
        gradients = stacked(odd, gm, go, head)
        outs, dqs, dks, dvs = [], [], [], []
        for block in range(CORES):
            prob = prob_ref[head * CORES + block]
            dscore = dscore_ref[head * CORES + block]
            outs.append(dot_first(prob, jnp.concatenate(values[block : block + 3], axis=0)))
            dqs.append(dot_first(dscore, jnp.concatenate(keys[block : block + 3], axis=0)))
            dks.append(dot(dscore[(2 - block) * rows :], queries[block]))
            dvs.append(dot(prob[(2 - block) * rows :], gradients[block]))
        for j in range(GROUP):
            at = slice(j * rows, (j + 1) * rows)
            put(odd, outm, outo, head * GROUP + j, outs[0][at], outs[1][at])
            put(odd, dqm, dqo, head * GROUP + j, dqs[0][at], dqs[1][at])
        put(odd, dkm, dko, head, dks[0] + dks[1][:rows], dks[1][rows:])
        put(odd, dvm, dvo, head, dvs[0] + dvs[1][:rows], dvs[1][rows:])


def join_kernel(rank_ref, *refs):
    count = len(refs) // 3
    odd = rank_ref[0] % 2
    for i in range(count):
        mine, other, target = refs[2 * i], refs[2 * i + 1], refs[2 * count + i]
        width = target.shape[1] // 2

        @pl.when(odd == 0)
        def _():
            target[:, :width] = mine[...]
            target[:, width:] = other[...]

        @pl.when(odd == 1)
        def _():
            target[:, width:] = mine[...]
            target[:, :width] = other[...]


def add_kernel(rank_ref, mine, other, backm, backo, target):
    odd = rank_ref[0] % 2
    width = target.shape[1] // 2

    @pl.when(odd == 0)
    def _():
        target[:, :width] = mine[...] + backm[...].astype(jnp.float32)
        target[:, width:] = other[...] + backo[...].astype(jnp.float32)

    @pl.when(odd == 1)
    def _():
        target[:, width:] = mine[...] + backm[...].astype(jnp.float32)
        target[:, :width] = other[...] + backo[...].astype(jnp.float32)


def shape(dims, dtype):
    return jax.ShapeDtypeStruct(dims, dtype)


def run(kernel, name, outputs, index, *operands):
    small = pl.BlockSpec(memory_space=pltpu.SMEM)
    whole = pl.BlockSpec(memory_space=pltpu.VMEM)
    return pl.pallas_call(
        kernel,
        in_specs=[small] + [whole] * len(operands),
        out_specs=[whole] * len(outputs),
        out_shape=outputs,
        compiler_params=pltpu.CompilerParams(vmem_limit_bytes=40 * 2**20),
        cost_estimate=pl.CostEstimate(flops=5000000000, bytes_accessed=1, transcendentals=0),
        name=name,
    )(index, *operands)


def on_device(queries, keys, values, output_gradient, doc_lengths):
    rows = queries.shape[0]
    devices = lax.axis_size(AXES)
    index = lax.axis_index(AXES).reshape(1)
    docs = doc_lengths.shape[0]

    ahead = [(r, (r + 2) % devices) for r in range(devices)]
    across = [(r, ((r + 2) % devices) ^ 1) for r in range(devices)]
    behind = [(there, here) for here, there in ahead]
    recross = [(there, here) for here, there in across]
    swap = [(r, r ^ 1) for r in range(devices)]

    def moved(value, pairs):
        return lax.ppermute(value, AXES, pairs)

    narrow = shape((rows, keys.shape[1] // CORES), jnp.bfloat16)
    wide = shape((rows, queries.shape[1] // CORES), jnp.bfloat16)
    narrow_sum = shape(narrow.shape, jnp.float32)
    wide_sum = shape(wide.shape, jnp.float32)
    pairs = shape((KEY_VALUE_HEADS, 3 * rows, GROUP * rows), jnp.bfloat16)

    km, kx = run(split_kernel, "split_keys", [narrow] * 2, index, keys)
    k2m, k2o = moved(km, ahead), moved(kx, across)
    vm, vx = run(split_kernel, "split_values", [narrow] * 2, index, values)
    v2m, v2o = moved(vm, ahead), moved(vx, across)
    qm, qx, gm, gx = run(split_kernel, "split_rows", [wide] * 4, index, queries, output_gradient)
    ko, vo, qo, go = (moved(x, swap) for x in (kx, vx, qx, gx))
    (bias,) = run(
        bias_kernel, "bias", [shape((CORES, 3 * rows, rows), jnp.float32)],
        index, doc_lengths.reshape(1, docs),
    )

    prob, dvm, dvo = run(
        value_kernel, "value_grads", [pairs, narrow, narrow],
        index, bias, qm, qo, gm, go, km, ko, k2m, k2o,
    )
    dv_back = moved(dvm, behind), moved(dvo, recross)
    dscore, dkm, dko = run(
        key_kernel, "key_grads", [pairs, narrow, narrow],
        index, prob, qm, qo, gm, go, vm, vo, v2m, v2o,
    )
    dk_back = moved(dkm, behind), moved(dko, recross)
    outm, outo, dqm, dqo, dkm, dko, dvm, dvo = run(
        rest_kernel, "other_grads",
        [wide, wide, wide_sum, wide_sum, narrow_sum, narrow_sum, narrow_sum, narrow_sum],
        index, prob, dscore, qm, qo, gm, go, km, ko, k2m, k2o, vm, vo, v2m, v2o,
    )
    outo, dqo, dko, dvo = (moved(x, swap) for x in (outo, dqo, dko, dvo))
    attended, dq = run(
        join_kernel, "join_rows",
        [shape(queries.shape, jnp.bfloat16), shape(queries.shape, jnp.float32)],
        index, outm, outo, dqm, dqo,
    )
    full = shape(keys.shape, jnp.float32)
    (dv,) = run(add_kernel, "join_values", [full], index, dvm, dvo, *dv_back)
    (dk,) = run(add_kernel, "join_keys", [full], index, dkm, dko, *dk_back)
    return attended, dq, dk, dv


def solution(mesh):
    split = P(AXES, None)
    return jax.shard_map(
        on_device,
        mesh=mesh,
        in_specs=(split, split, split, split, P()),
        out_specs=(split, split, split, split),
        check_vma=False,
    )
```

```python
import functools

import jax
import jax.numpy as jnp
from jax import lax
from jax.experimental import pallas as pl
from jax.experimental.pallas import tpu as pltpu
from jax.sharding import PartitionSpec as P

QUERY_HEADS = 16
KEY_VALUE_HEADS = 8
HEAD_SIZE = 128
LOCAL_WINDOW = 256
GROUP = QUERY_HEADS // KEY_VALUE_HEADS
CORES = 2
CORE_HEADS = KEY_VALUE_HEADS // CORES
CORE_QUERIES = QUERY_HEADS // CORES
AT_GRADIENTS = CORE_QUERIES
AT_KEYS = 2 * CORE_QUERIES
AT_VALUES = AT_KEYS + CORE_HEADS
ALL_SENT = AT_VALUES + CORE_HEADS
AXES = ("dp", "seq")

score_scale = 168.0 ** (-0.5)
LOG2E = 1.4426950408889634
NEGATIVE = -1e30

CONTRACT_LAST = (((1,), (1,)), ((), ()))
CONTRACT_FIRST = (((0,), (0,)), ((), ()))


COST = {"far_keys": 20000, "own_values": 20000}


def dot(a, b):
    return jnp.dot(a, b, preferred_element_type=jnp.float32)


def dot_last(a, b):
    return lax.dot_general(a, b, CONTRACT_LAST, preferred_element_type=jnp.float32)


def dot_first(a, b):
    return lax.dot_general(a, b, CONTRACT_FIRST, preferred_element_type=jnp.float32)


def span(head):
    return slice(head * HEAD_SIZE, (head + 1) * HEAD_SIZE)


def both(odd, mine, other, head, offset=0):
    a, b = mine[:, span(head)], other[:, span(offset + head)]
    return jnp.where(odd, b, a), jnp.where(odd, a, b)


def stacked(odd, mine, other, head, offset):
    pieces = [both(odd, mine, other, head * GROUP + j, offset) for j in range(GROUP)]
    return [jnp.concatenate([piece[block] for piece in pieces], axis=0) for block in range(CORES)]


def put(odd, mine, other, head, first, second, offset=0):
    mine[:, span(head)] = jnp.where(odd, second, first).astype(mine.dtype)
    other[:, span(offset + head)] = jnp.where(odd, first, second).astype(other.dtype)


def split_kernel(rank_ref, source, mine, other):
    odd = rank_ref[0] % 2
    width = source.shape[1] // CORES
    for core in range(CORES):

        @pl.when(odd == core)
        def _():
            mine[...] = source[:, core * width : (core + 1) * width]
            other[...] = source[:, (1 - core) * width : (2 - core) * width]


def rows_kernel(rank_ref, q_ref, g_ref, v_ref, kx, qm, gm, vm, vx, sent):
    odd = rank_ref[0] % 2
    wide, narrow = qm.shape[1], vm.shape[1]
    at_keys, at_values = AT_KEYS * HEAD_SIZE, AT_VALUES * HEAD_SIZE
    for core in range(CORES):
        here = slice(core * wide, (core + 1) * wide)
        there = slice((1 - core) * wide, (2 - core) * wide)

        @pl.when(odd == core)
        def _():
            qm[...] = q_ref[:, here]
            gm[...] = g_ref[:, here]
            sent[:, :wide] = q_ref[:, there]
            sent[:, wide : 2 * wide] = g_ref[:, there]
            vm[...] = v_ref[:, core * narrow : (core + 1) * narrow]
            vx[...] = v_ref[:, (1 - core) * narrow : (2 - core) * narrow]
            sent[:, at_values:] = v_ref[:, (1 - core) * narrow : (2 - core) * narrow]

    sent[:, at_keys:at_values] = kx[...]


def bias_kernel(rank_ref, lens_ref, bias_ref):
    _, span_rows, rows = bias_ref.shape
    docs = lens_ref.shape[1]
    later = lax.broadcasted_iota(jnp.int32, (docs, docs), 0)
    earlier = lax.broadcasted_iota(jnp.int32, (docs, docs), 1)
    lens = jnp.broadcast_to(lens_ref[...].astype(jnp.float32), (docs, docs))
    ends = jnp.sum(jnp.where(earlier <= later, lens, 0.0), axis=1, keepdims=True)
    for block in range(CORES):
        first = (rank_ref[0] // CORES * CORES + block) * rows
        query = first + lax.broadcasted_iota(jnp.int32, (1, rows), 1)
        ended = jnp.where(ends <= query.astype(jnp.float32), ends, 0.0)
        start = jnp.max(ended, axis=0, keepdims=True).astype(jnp.int32)
        lowest = jnp.maximum(start, query - (LOCAL_WINDOW - 1))
        key = first - 2 * rows + lax.broadcasted_iota(jnp.int32, (span_rows, rows), 0)
        bias_ref[block] = jnp.where((key >= lowest) & (key <= query), 0.0, NEGATIVE)


def order_kernel(rank_ref, mine, other, first, second):
    odd = rank_ref[0] % 2
    for core in range(CORES):

        @pl.when(odd == core)
        def _():
            (second if core else first)[...] = mine[...]
            (first if core else second)[...] = other[...]


def value_kernel(
    rank_ref, bias_ref, qm, gm, km, near, ka, kb,
    prob_ref, dvm, dvo,
):
    rows = qm.shape[0]
    odd = rank_ref[0] % 2 == 1
    for head in range(CORE_HEADS):
        blocks = (ka[:, span(head)], kb[:, span(head)]) + both(odd, km, near, head, AT_KEYS)
        queries = stacked(odd, qm, near, head, 0)
        gradients = stacked(odd, gm, near, head, AT_GRADIENTS)
        grads = []
        for block in range(CORES):
            keys = jnp.concatenate(blocks[block : block + 3], axis=0)
            bias = jnp.concatenate([bias_ref[block]] * GROUP, axis=1)
            scores = dot_last(keys, queries[block]) * (score_scale * LOG2E) + bias
            top = jnp.max(scores, axis=0, keepdims=True)
            raised = jnp.exp2(scores - top)
            total = jnp.sum(raised, axis=0, keepdims=True)
            prob = (raised * (1.0 / total)).astype(jnp.bfloat16)
            prob_ref[head * CORES + block] = prob
            grads.append(dot(prob[: (2 - block) * rows], gradients[block]))
        put(odd, dvm, dvo, head, grads[0][:rows], grads[0][rows:] + grads[1])


def local_sum(core, pairs_ref, sources, head, rows):
    at = head * CORES + core
    total = dot(pairs_ref[at, 2 * rows :], sources[core])
    if core == 0:
        total += dot(pairs_ref[at + 1, rows : 2 * rows], sources[1])
    return total


def local_grads(core, prob_ref, dscore_ref, keys, values, queries, head, rows):
    at = head * CORES + core
    out = dot_first(prob_ref[at], jnp.concatenate(values[core : core + 3], axis=0))
    dq = dot_first(dscore_ref[at], jnp.concatenate(keys[core : core + 3], axis=0))
    dk = local_sum(core, dscore_ref, queries, head, rows)
    return out, dq, dk


def key_kernel(
    rank_ref, prob_ref, qm, gm, km, vm, near, ka, kb, v2m, v2o,
    dscore_ref, dkm, dko, sent,
):
    rows = qm.shape[0]
    odd = rank_ref[0] % 2 == 1
    for head in range(CORE_HEADS):
        values = both(odd, v2m, v2o, head) + both(odd, vm, near, head, AT_VALUES)
        queries = stacked(odd, qm, near, head, 0)
        gradients = stacked(odd, gm, near, head, AT_GRADIENTS)
        grads = []
        for block in range(CORES):
            dprob = dot_last(jnp.concatenate(values[block : block + 3], axis=0), gradients[block])
            prob = prob_ref[head * CORES + block].astype(jnp.float32)
            delta = jnp.sum(prob * dprob, axis=0, keepdims=True)
            dscore = (prob * ((dprob - delta) * score_scale)).astype(jnp.bfloat16)
            dscore_ref[head * CORES + block] = dscore
            grads.append(dot(dscore[: (2 - block) * rows], queries[block]))
        put(odd, dkm, dko, head, grads[0][:rows], grads[0][rows:] + grads[1])
    for core in range(CORES):

        @pl.when(rank_ref[0] % 2 != core)
        def _():
            for head in range(CORE_HEADS):
                keys = (ka[:, span(head)], kb[:, span(head)]) + both(odd, km, near, head, AT_KEYS)
                values = both(odd, v2m, v2o, head) + both(odd, vm, near, head, AT_VALUES)
                queries = stacked(odd, qm, near, head, 0)
                gradients = stacked(odd, gm, near, head, AT_GRADIENTS)
                out, dq, dk = local_grads(core, prob_ref, dscore_ref, keys, values, queries, head, rows)
                for j in range(GROUP):
                    at = slice(j * rows, (j + 1) * rows)
                    sent[:, span(head * GROUP + j)] = out[at].astype(jnp.bfloat16)
                    sent[:, span(AT_GRADIENTS + head * GROUP + j)] = dq[at].astype(jnp.bfloat16)
                sent[:, span(AT_KEYS + head)] = dk.astype(jnp.bfloat16)
                dv = local_sum(core, prob_ref, gradients, head, rows)
                sent[:, span(AT_VALUES + head)] = dv.astype(jnp.bfloat16)


def own_values_kernel(rank_ref, prob_ref, gm, near, backm, dvm):
    rows = gm.shape[0]
    odd = rank_ref[0] % 2 == 1
    for core in range(CORES):

        @pl.when(rank_ref[0] % 2 == core)
        def _():
            for head in range(CORE_HEADS):
                gradients = stacked(odd, gm, near, head, AT_GRADIENTS)
                dv = local_sum(core, prob_ref, gradients, head, rows)
                dvm[:, span(head)] = dv + backm[:, span(head)].astype(jnp.float32)


def rows_grads_kernel(
    rank_ref, prob_ref, dscore_ref, qm, gm, km, vm, near, ka, kb, v2m, v2o, got, dvm, backo,
    out_ref, dq_ref, dkm, dv_ref,
):
    rows = qm.shape[0]
    odd = rank_ref[0] % 2 == 1
    wide, narrow = qm.shape[1], km.shape[1]
    for core in range(CORES):

        @pl.when(rank_ref[0] % 2 == core)
        def _():
            there = slice((1 - core) * wide, (2 - core) * wide)
            out_ref[:, there] = got[:, :wide]
            dq_ref[:, there] = got[:, wide : 2 * wide].astype(jnp.float32)
            dv_ref[:, core * narrow : (core + 1) * narrow] = dvm[...]
            dv_ref[:, (1 - core) * narrow : (2 - core) * narrow] = backo[...].astype(jnp.float32) + got[
                :, AT_VALUES * HEAD_SIZE :
            ].astype(jnp.float32)
            for head in range(CORE_HEADS):
                keys = (ka[:, span(head)], kb[:, span(head)]) + both(odd, km, near, head, AT_KEYS)
                values = both(odd, v2m, v2o, head) + both(odd, vm, near, head, AT_VALUES)
                queries = stacked(odd, qm, near, head, 0)
                out, dq, dk = local_grads(core, prob_ref, dscore_ref, keys, values, queries, head, rows)
                for j in range(GROUP):
                    at = slice(j * rows, (j + 1) * rows)
                    here = span(core * CORE_QUERIES + head * GROUP + j)
                    out_ref[:, here] = out[at].astype(jnp.bfloat16)
                    dq_ref[:, here] = dq[at]
                dkm[:, span(head)] = dk


def add_kernel(offset, rank_ref, mine, near, backm, backo, target):
    odd = rank_ref[0] % 2
    width = mine.shape[1]
    offset = offset * HEAD_SIZE
    for core in range(CORES):
        here = slice(core * width, (core + 1) * width)
        there = slice((1 - core) * width, (2 - core) * width)

        @pl.when(odd == core)
        def _():
            target[:, here] = mine[...] + backm[...].astype(jnp.float32)
            target[:, there] = near[:, offset : offset + width].astype(jnp.float32) + backo[...].astype(jnp.float32)


def shape(dims, dtype):
    return jax.ShapeDtypeStruct(dims, dtype)


def run(kernel, name, outputs, index, *operands):
    small = pl.BlockSpec(memory_space=pltpu.SMEM)
    whole = pl.BlockSpec(memory_space=pltpu.VMEM)
    return pl.pallas_call(
        kernel,
        in_specs=[small] + [whole] * len(operands),
        out_specs=[whole] * len(outputs),
        out_shape=outputs,
        compiler_params=pltpu.CompilerParams(vmem_limit_bytes=40 * 2**20),
        cost_estimate=pl.CostEstimate(flops=COST.get(name, 0) * 1000000, bytes_accessed=1000, transcendentals=0),
        name=name,
    )(index, *operands)


def on_device(queries, keys, values, output_gradient, doc_lengths):
    rows = queries.shape[0]
    devices = lax.axis_size(AXES)
    index = lax.axis_index(AXES).reshape(1)
    docs = doc_lengths.shape[0]

    ahead = [(r, (r + 2) % devices) for r in range(devices)]
    across = [(r, ((r + 2) % devices) ^ 1) for r in range(devices)]
    behind = [(there, here) for here, there in ahead]
    recross = [(there, here) for here, there in across]
    swap = [(r, r ^ 1) for r in range(devices)]

    def moved(value, pairs):
        return lax.ppermute(value, AXES, pairs)

    narrow = shape((rows, keys.shape[1] // CORES), jnp.bfloat16)
    wide = shape((rows, queries.shape[1] // CORES), jnp.bfloat16)
    narrow_sum = shape(narrow.shape, jnp.float32)
    wide_sum = shape(wide.shape, jnp.float32)
    pairs = shape((KEY_VALUE_HEADS, 3 * rows, GROUP * rows), jnp.bfloat16)

    full = shape(keys.shape, jnp.float32)
    all_sent = shape((rows, ALL_SENT * HEAD_SIZE), jnp.bfloat16)
    km, kx = run(split_kernel, "split_keys", [narrow] * 2, index, keys)
    k2m, k2o = moved(km, ahead), moved(kx, across)
    qm, gm, vm, vx, sent = run(
        rows_kernel, "split_rows", [wide, wide, narrow, narrow, all_sent],
        index, queries, output_gradient, values, kx,
    )
    v2m, v2o = moved(vm, ahead), moved(vx, across)
    near = moved(sent, swap)
    (bias,) = run(
        bias_kernel, "bias", [shape((CORES, 3 * rows, rows), jnp.float32)],
        index, doc_lengths.reshape(1, docs),
    )
    ka, kb = run(order_kernel, "far_keys", [narrow] * 2, index, k2m, k2o)
    prob, dvm, dvo = run(
        value_kernel, "value_grads", [pairs, narrow, narrow],
        index, bias, qm, gm, km, near, ka, kb,
    )
    dv_back = moved(dvm, behind), moved(dvo, recross)
    dscore, dkm, dko, sent = run(
        key_kernel, "key_grads", [pairs, narrow, narrow, all_sent],
        index, prob, qm, gm, km, vm, near, ka, kb, v2m, v2o,
    )
    dk_back = moved(dkm, behind), moved(dko, recross)
    got = moved(sent, swap)
    (dvm,) = run(
        own_values_kernel, "own_values", [narrow_sum], index, prob, gm, near, dv_back[0]
    )
    got, dvm = lax.optimization_barrier((got, dvm))
    attended, dq, dkm, dv = run(
        rows_grads_kernel, "other_grads",
        [shape(queries.shape, jnp.bfloat16), shape(queries.shape, jnp.float32), narrow_sum, full],
        index, prob, dscore, qm, gm, km, vm, near, ka, kb, v2m, v2o, got, dvm, dv_back[1],
    )
    (dk,) = run(functools.partial(add_kernel, AT_KEYS), "join_keys", [full], index, dkm, got, *dk_back)
    return attended, dq, dk, dv


def solution(mesh):
    split = P(AXES, None)
    return jax.shard_map(
        on_device,
        mesh=mesh,
        in_specs=(split, split, split, split, P()),
        out_specs=(split, split, split, split),
        check_vma=False,
    )
```

```python
import functools

import jax
import jax.numpy as jnp
from jax import lax
from jax.experimental import pallas as pl
from jax.experimental.pallas import tpu as pltpu
from jax.sharding import PartitionSpec as P

QUERY_HEADS = 16
KEY_VALUE_HEADS = 8
HEAD_SIZE = 128
LOCAL_WINDOW = 256
GROUP = QUERY_HEADS // KEY_VALUE_HEADS
CORES = 2
CORE_HEADS = KEY_VALUE_HEADS // CORES
CORE_QUERIES = QUERY_HEADS // CORES
AT_GRADIENTS = CORE_QUERIES
AT_KEYS = 2 * CORE_QUERIES
AT_VALUES = AT_KEYS + CORE_HEADS
ALL_SENT = AT_VALUES + CORE_HEADS
AXES = ("dp", "seq")

score_scale = 168.0 ** (-0.5)
LOG2E = 1.4426950408889634
NEGATIVE = -1e30

CONTRACT_LAST = (((1,), (1,)), ((), ()))
CONTRACT_FIRST = (((0,), (0,)), ((), ()))


COST = {"split_keys": 20000, "far_keys": 20000, "own_values": 20000}


def dot(a, b):
    return jnp.dot(a, b, preferred_element_type=jnp.float32)


def dot_last(a, b):
    return lax.dot_general(a, b, CONTRACT_LAST, preferred_element_type=jnp.float32)


def dot_first(a, b):
    return lax.dot_general(a, b, CONTRACT_FIRST, preferred_element_type=jnp.float32)


def span(head):
    return slice(head * HEAD_SIZE, (head + 1) * HEAD_SIZE)


def both(odd, mine, other, head, offset=0):
    a, b = mine[:, span(head)], other[:, span(offset + head)]
    return jnp.where(odd, b, a), jnp.where(odd, a, b)


def stacked(odd, mine, other, head, offset):
    pieces = [both(odd, mine, other, head * GROUP + j, offset) for j in range(GROUP)]
    return [jnp.concatenate([piece[block] for piece in pieces], axis=0) for block in range(CORES)]


def put(odd, mine, other, head, first, second, offset=0):
    mine[:, span(head)] = jnp.where(odd, second, first).astype(mine.dtype)
    other[:, span(offset + head)] = jnp.where(odd, first, second).astype(other.dtype)


def halves(odd, width):
    return (
        pl.ds(pl.multiple_of(odd * width, width), width),
        pl.ds(pl.multiple_of((1 - odd) * width, width), width),
    )


def copied(pairs, sem):
    copies = [pltpu.make_async_copy(source, target, sem.at[i]) for i, (source, target) in enumerate(pairs)]
    for copy in copies:
        copy.start()
    return copies


def split_kernel(rank_ref, source, mine, other, sem):
    here, there = halves(rank_ref[0] % CORES, mine.shape[1])
    for copy in copied([(source.at[:, here], mine), (source.at[:, there], other)], sem):
        copy.wait()


def fill_bias(rank, lens_ref, bias_ref):
    _, span_rows, rows = bias_ref.shape
    docs = lens_ref.shape[1]
    later = lax.broadcasted_iota(jnp.int32, (docs, docs), 0)
    earlier = lax.broadcasted_iota(jnp.int32, (docs, docs), 1)
    lens = jnp.broadcast_to(lens_ref[...].astype(jnp.float32), (docs, docs))
    ends = jnp.sum(jnp.where(earlier <= later, lens, 0.0), axis=1, keepdims=True)
    for block in range(CORES):
        first = (rank // CORES * CORES + block) * rows
        query = first + lax.broadcasted_iota(jnp.int32, (1, rows), 1)
        ended = jnp.where(ends <= query.astype(jnp.float32), ends, 0.0)
        start = jnp.max(ended, axis=0, keepdims=True).astype(jnp.int32)
        lowest = jnp.maximum(start, query - (LOCAL_WINDOW - 1))
        key = first - 2 * rows + lax.broadcasted_iota(jnp.int32, (span_rows, rows), 0)
        bias_ref[block] = jnp.where((key >= lowest) & (key <= query), 0.0, NEGATIVE)


def rows_kernel(
    rank_ref, lens_ref, q_ref, g_ref, k_ref, v_ref, qm, gm, vm, vx, sent, bias_ref, sem
):
    odd = rank_ref[0] % CORES
    wide, narrow = qm.shape[1], vm.shape[1]
    here, there = halves(odd, wide)
    here_kv, there_kv = halves(odd, narrow)
    at_keys, at_values = AT_KEYS * HEAD_SIZE, AT_VALUES * HEAD_SIZE
    copies = copied(
        [
            (v_ref.at[:, here_kv], vm),
            (v_ref.at[:, there_kv], vx),
            (q_ref.at[:, there], sent.at[:, :wide]),
            (g_ref.at[:, there], sent.at[:, wide : 2 * wide]),
            (k_ref.at[:, there_kv], sent.at[:, at_keys:at_values]),
            (v_ref.at[:, there_kv], sent.at[:, at_values:]),
            (q_ref.at[:, here], qm),
            (g_ref.at[:, here], gm),
        ],
        sem,
    )
    fill_bias(rank_ref[0], lens_ref, bias_ref)
    for copy in copies:
        copy.wait()


def order_kernel(rank_ref, mine, other, first, second):
    odd = rank_ref[0] % 2
    for core in range(CORES):

        @pl.when(odd == core)
        def _():
            (second if core else first)[...] = mine[...]
            (first if core else second)[...] = other[...]


def staged(units, *stages):
    held = {}
    for step in range(len(units) + len(stages) - 1):
        for depth, stage in enumerate(stages):
            at = step - depth
            if 0 <= at < len(units):
                held[at] = stage(*units[at], *held.get(at, ()))


UNITS = [(head, block) for head in range(CORE_HEADS) for block in range(CORES)]


def value_kernel(
    rank_ref, bias_ref, qm, gm, km, near, ka, kb,
    prob_ref, dvm, dvo,
):
    rows = qm.shape[0]
    odd = rank_ref[0] % 2 == 1
    grads = {}

    def score(head, block):
        blocks = (ka[:, span(head)], kb[:, span(head)]) + both(odd, km, near, head, AT_KEYS)
        queries = stacked(odd, qm, near, head, 0)[block]
        return (dot_last(jnp.concatenate(blocks[block : block + 3], axis=0), queries),)

    def normalise(head, block, scores):
        bias = jnp.concatenate([bias_ref[block]] * GROUP, axis=1)
        scores = scores * (score_scale * LOG2E) + bias
        top = jnp.max(scores, axis=0, keepdims=True)
        raised = jnp.exp2(scores - top)
        total = jnp.sum(raised, axis=0, keepdims=True)
        prob = (raised * (1.0 / total)).astype(jnp.bfloat16)
        prob_ref[head * CORES + block] = prob
        return (prob[: (2 - block) * rows],)

    def far_grads(head, block, prob):
        grads[block] = dot(prob, stacked(odd, gm, near, head, AT_GRADIENTS)[block])
        if block == 1:
            put(odd, dvm, dvo, head, grads[0][:rows], grads[0][rows:] + grads[1])
        return ()

    staged(UNITS, score, lambda head, block, scores: (scores,), normalise, far_grads)


def local_sum(core, pairs_ref, sources, head, rows):
    at = head * CORES + core
    total = dot(pairs_ref[at, 2 * rows :], sources[core])
    if core == 0:
        total += dot(pairs_ref[at + 1, rows : 2 * rows], sources[1])
    return total


def local_grads(core, prob_ref, dscore_ref, keys, values, queries, head, rows):
    at = head * CORES + core
    out = dot_first(prob_ref[at], jnp.concatenate(values[core : core + 3], axis=0))
    dq = dot_first(dscore_ref[at], jnp.concatenate(keys[core : core + 3], axis=0))
    dk = local_sum(core, dscore_ref, queries, head, rows)
    return out, dq, dk


def chosen(odd, pieces):
    return jnp.concatenate([jnp.where(odd, pieces[i], pieces[i + 1]) for i in range(3)], axis=0)


def other_sum(odd, pairs_ref, sources, head, rows):
    here = head * CORES
    mine = jnp.where(odd, sources[0], sources[1])
    total = dot(pairs_ref[here + jnp.where(odd, 0, 1), 2 * rows :], mine)
    return total + jnp.where(odd, dot(pairs_ref[here + 1, rows : 2 * rows], sources[1]), 0.0)


def key_kernel(
    rank_ref, prob_ref, qm, gm, km, vm, near, ka, kb, v2m, v2o,
    dscore_ref, dkm, dko, sent,
):
    rows = qm.shape[0]
    odd = rank_ref[0] % 2 == 1
    grads = {}

    def value_blocks(head):
        return both(odd, v2m, v2o, head) + both(odd, vm, near, head, AT_VALUES)

    def product(head, block):
        gradients = stacked(odd, gm, near, head, AT_GRADIENTS)[block]
        values = jnp.concatenate(value_blocks(head)[block : block + 3], axis=0)
        return (dot_last(values, gradients),)

    def scale(head, block, dprob):
        at = head * CORES + block
        prob = prob_ref[at].astype(jnp.float32)
        delta = jnp.sum(prob * dprob, axis=0, keepdims=True)
        dscore = (prob * ((dprob - delta) * score_scale)).astype(jnp.bfloat16)
        dscore_ref[at] = dscore
        return (dscore[: (2 - block) * rows],)

    def far_grads(head, block, dscore):
        grads[block] = dot(dscore, stacked(odd, qm, near, head, 0)[block])
        if block == 1:
            put(odd, dkm, dko, head, grads[0][:rows], grads[0][rows:] + grads[1])
            send(head)
        return ()

    def send(head):
        keys = (ka[:, span(head)], kb[:, span(head)]) + both(odd, km, near, head, AT_KEYS)
        at = head * CORES + jnp.where(odd, 0, 1)
        out = dot_first(prob_ref[at], chosen(odd, value_blocks(head)))
        dq = dot_first(dscore_ref[at], chosen(odd, keys))
        for j in range(GROUP):
            piece = slice(j * rows, (j + 1) * rows)
            sent[:, span(head * GROUP + j)] = out[piece].astype(jnp.bfloat16)
            sent[:, span(AT_GRADIENTS + head * GROUP + j)] = dq[piece].astype(jnp.bfloat16)
        dk = other_sum(odd, dscore_ref, stacked(odd, qm, near, head, 0), head, rows)
        dv = other_sum(odd, prob_ref, stacked(odd, gm, near, head, AT_GRADIENTS), head, rows)
        sent[:, span(AT_KEYS + head)] = dk.astype(jnp.bfloat16)
        sent[:, span(AT_VALUES + head)] = dv.astype(jnp.bfloat16)

    staged(UNITS, product, lambda head, block, dprob: (dprob,), scale, far_grads)


def own_values_kernel(rank_ref, prob_ref, gm, near, backm, dvm):
    rows = gm.shape[0]
    odd = rank_ref[0] % 2 == 1
    for core in range(CORES):

        @pl.when(rank_ref[0] % 2 == core)
        def _():
            for head in range(CORE_HEADS):
                gradients = stacked(odd, gm, near, head, AT_GRADIENTS)
                dv = local_sum(core, prob_ref, gradients, head, rows)
                dvm[:, span(head)] = dv + backm[:, span(head)].astype(jnp.float32)


def rows_grads_kernel(
    rank_ref, prob_ref, dscore_ref, qm, gm, km, vm, near, ka, kb, v2m, v2o, got, dvm, backo,
    out_ref, dq_ref, dkm, dv_ref,
):
    rows = qm.shape[0]
    odd = rank_ref[0] % 2 == 1
    wide, narrow = qm.shape[1], km.shape[1]
    for core in range(CORES):

        @pl.when(rank_ref[0] % 2 == core)
        def _():
            there = slice((1 - core) * wide, (2 - core) * wide)
            out_ref[:, there] = got[:, :wide]
            dq_ref[:, there] = got[:, wide : 2 * wide].astype(jnp.float32)
            dv_ref[:, core * narrow : (core + 1) * narrow] = dvm[...]
            dv_ref[:, (1 - core) * narrow : (2 - core) * narrow] = backo[...].astype(jnp.float32) + got[
                :, AT_VALUES * HEAD_SIZE :
            ].astype(jnp.float32)
            for head in range(CORE_HEADS):
                keys = (ka[:, span(head)], kb[:, span(head)]) + both(odd, km, near, head, AT_KEYS)
                values = both(odd, v2m, v2o, head) + both(odd, vm, near, head, AT_VALUES)
                queries = stacked(odd, qm, near, head, 0)
                out, dq, dk = local_grads(core, prob_ref, dscore_ref, keys, values, queries, head, rows)
                for j in range(GROUP):
                    at = slice(j * rows, (j + 1) * rows)
                    here = span(core * CORE_QUERIES + head * GROUP + j)
                    out_ref[:, here] = out[at].astype(jnp.bfloat16)
                    dq_ref[:, here] = dq[at]
                dkm[:, span(head)] = dk


def add_kernel(offset, rank_ref, mine, near, backm, backo, target):
    odd = rank_ref[0] % 2
    width = mine.shape[1]
    offset = offset * HEAD_SIZE
    for core in range(CORES):
        here = slice(core * width, (core + 1) * width)
        there = slice((1 - core) * width, (2 - core) * width)

        @pl.when(odd == core)
        def _():
            target[:, here] = mine[...] + backm[...].astype(jnp.float32)
            target[:, there] = near[:, offset : offset + width].astype(jnp.float32) + backo[...].astype(jnp.float32)


def shape(dims, dtype):
    return jax.ShapeDtypeStruct(dims, dtype)


def run(kernel, name, outputs, index, *operands, far=(), scratch=()):
    small = pl.BlockSpec(memory_space=pltpu.SMEM)
    whole = pl.BlockSpec(memory_space=pltpu.VMEM)
    there = pl.BlockSpec(memory_space=pltpu.HBM)
    return pl.pallas_call(
        kernel,
        in_specs=[small] + [there if i in far else whole for i in range(len(operands))],
        out_specs=[whole] * len(outputs),
        out_shape=outputs,
        scratch_shapes=scratch,
        compiler_params=pltpu.CompilerParams(vmem_limit_bytes=40 * 2**20),
        cost_estimate=pl.CostEstimate(flops=COST.get(name, 0) * 1000000, bytes_accessed=1000, transcendentals=0),
        name=name,
    )(index, *operands)


def on_device(queries, keys, values, output_gradient, doc_lengths):
    rows = queries.shape[0]
    devices = lax.axis_size(AXES)
    index = lax.axis_index(AXES).reshape(1)
    docs = doc_lengths.shape[0]

    ahead = [(r, (r + 2) % devices) for r in range(devices)]
    across = [(r, ((r + 2) % devices) ^ 1) for r in range(devices)]
    behind = [(there, here) for here, there in ahead]
    recross = [(there, here) for here, there in across]
    swap = [(r, r ^ 1) for r in range(devices)]

    def moved(value, pairs):
        return lax.ppermute(value, AXES, pairs)

    narrow = shape((rows, keys.shape[1] // CORES), jnp.bfloat16)
    wide = shape((rows, queries.shape[1] // CORES), jnp.bfloat16)
    narrow_sum = shape(narrow.shape, jnp.float32)
    wide_sum = shape(wide.shape, jnp.float32)
    pairs = shape((KEY_VALUE_HEADS, 3 * rows, GROUP * rows), jnp.bfloat16)

    full = shape(keys.shape, jnp.float32)
    all_sent = shape((rows, ALL_SENT * HEAD_SIZE), jnp.bfloat16)
    def copies(count):
        return [pltpu.SemaphoreType.DMA((count,))]

    km, kx = run(split_kernel, "split_keys", [narrow] * 2, index, keys, far=(0,), scratch=copies(2))
    k2m, k2o = moved(km, ahead), moved(kx, across)
    queries, kx = lax.optimization_barrier((queries, kx))
    qm, gm, vm, vx, sent, bias = run(
        rows_kernel, "split_rows",
        [wide, wide, narrow, narrow, all_sent, shape((CORES, 3 * rows, rows), jnp.float32)],
        index, doc_lengths.reshape(1, docs), queries, output_gradient, keys, values,
        far=(1, 2, 3, 4), scratch=copies(8),
    )
    v2m, v2o = moved(vm, ahead), moved(vx, across)
    near = moved(sent, swap)
    ka, kb = run(order_kernel, "far_keys", [narrow] * 2, index, k2m, k2o)
    prob, dvm, dvo = run(
        value_kernel, "value_grads", [pairs, narrow, narrow],
        index, bias, qm, gm, km, near, ka, kb,
    )
    dvm, v2o = lax.optimization_barrier((dvm, v2o))
    dv_back = moved(dvm, behind), moved(dvo, recross)
    dscore, dkm, dko, sent = run(
        key_kernel, "key_grads", [pairs, narrow, narrow, all_sent],
        index, prob, qm, gm, km, vm, near, ka, kb, v2m, v2o,
    )
    dk_back = moved(dkm, behind), moved(dko, recross)
    got = moved(sent, swap)
    (dvm,) = run(
        own_values_kernel, "own_values", [narrow_sum], index, prob, gm, near, dv_back[0]
    )
    got, dvm = lax.optimization_barrier((got, dvm))
    attended, dq, dkm, dv = run(
        rows_grads_kernel, "other_grads",
        [shape(queries.shape, jnp.bfloat16), shape(queries.shape, jnp.float32), narrow_sum, full],
        index, prob, dscore, qm, gm, km, vm, near, ka, kb, v2m, v2o, got, dvm, dv_back[1],
    )
    (dk,) = run(functools.partial(add_kernel, AT_KEYS), "join_keys", [full], index, dkm, got, *dk_back)
    return attended, dq, dk, dv


def solution(mesh):
    split = P(AXES, None)
    return jax.shard_map(
        on_device,
        mesh=mesh,
        in_specs=(split, split, split, split, P()),
        out_specs=(split, split, split, split),
        check_vma=False,
    )
```

```python
import functools

import jax
import jax.numpy as jnp
from jax import lax
from jax.experimental import pallas as pl
from jax.experimental.pallas import tpu as pltpu
from jax.sharding import PartitionSpec as P

QUERY_HEADS = 16
KEY_VALUE_HEADS = 8
HEAD_SIZE = 128
LOCAL_WINDOW = 256
GROUP = QUERY_HEADS // KEY_VALUE_HEADS
CORES = 2
CORE_HEADS = KEY_VALUE_HEADS // CORES
CORE_QUERIES = QUERY_HEADS // CORES
AT_GRADIENTS = CORE_QUERIES
AT_KEYS = 2 * CORE_QUERIES
AT_VALUES = AT_KEYS + CORE_HEADS
ALL_SENT = AT_VALUES + CORE_HEADS
AXES = ("dp", "seq")

score_scale = 168.0 ** (-0.5)
LOG2E = 1.4426950408889634
NEGATIVE = -1e30

CONTRACT_LAST = (((1,), (1,)), ((), ()))
CONTRACT_FIRST = (((0,), (0,)), ((), ()))


COST = {"own_grads": 20000, "split_keys": 20000, "far_keys": 20000}


def dot(a, b):
    return jnp.dot(a, b, preferred_element_type=jnp.float32)


def dot_last(a, b):
    return lax.dot_general(a, b, CONTRACT_LAST, preferred_element_type=jnp.float32)


def dot_first(a, b):
    return lax.dot_general(a, b, CONTRACT_FIRST, preferred_element_type=jnp.float32)


def span(head):
    return slice(head * HEAD_SIZE, (head + 1) * HEAD_SIZE)


def both(odd, mine, other, head, offset=0):
    a, b = mine[:, span(head)], other[:, span(offset + head)]
    return jnp.where(odd, b, a), jnp.where(odd, a, b)


def stacked(odd, mine, other, head, offset):
    pieces = [both(odd, mine, other, head * GROUP + j, offset) for j in range(GROUP)]
    return [jnp.concatenate([piece[block] for piece in pieces], axis=0) for block in range(CORES)]


def put(odd, mine, other, head, first, second, offset=0):
    mine[:, span(head)] = jnp.where(odd, second, first).astype(mine.dtype)
    other[:, span(offset + head)] = jnp.where(odd, first, second).astype(other.dtype)


def halves(odd, width):
    return (
        pl.ds(pl.multiple_of(odd * width, width), width),
        pl.ds(pl.multiple_of((1 - odd) * width, width), width),
    )


def copied(pairs, sem):
    copies = [pltpu.make_async_copy(source, target, sem.at[i]) for i, (source, target) in enumerate(pairs)]
    for copy in copies:
        copy.start()
    return copies


def split_kernel(rank_ref, source, mine, other, sem):
    here, there = halves(rank_ref[0] % CORES, mine.shape[1])
    for copy in copied([(source.at[:, here], mine), (source.at[:, there], other)], sem):
        copy.wait()


def fill_bias(rank, lens_ref, bias_ref):
    _, span_rows, rows = bias_ref.shape
    docs = lens_ref.shape[1]
    later = lax.broadcasted_iota(jnp.int32, (docs, docs), 0)
    earlier = lax.broadcasted_iota(jnp.int32, (docs, docs), 1)
    lens = jnp.broadcast_to(lens_ref[...].astype(jnp.float32), (docs, docs))
    ends = jnp.sum(jnp.where(earlier <= later, lens, 0.0), axis=1, keepdims=True)
    for block in range(CORES):
        first = (rank // CORES * CORES + block) * rows
        query = first + lax.broadcasted_iota(jnp.int32, (1, rows), 1)
        ended = jnp.where(ends <= query.astype(jnp.float32), ends, 0.0)
        start = jnp.max(ended, axis=0, keepdims=True).astype(jnp.int32)
        lowest = jnp.maximum(start, query - (LOCAL_WINDOW - 1))
        key = first - 2 * rows + lax.broadcasted_iota(jnp.int32, (span_rows, rows), 0)
        bias_ref[block] = jnp.where((key >= lowest) & (key <= query), 0.0, NEGATIVE)


def rows_kernel(
    rank_ref, lens_ref, q_ref, g_ref, k_ref, v_ref, qm, gm, vm, vx, sent, bias_ref, sem
):
    odd = rank_ref[0] % CORES
    wide, narrow = qm.shape[1], vm.shape[1]
    here, there = halves(odd, wide)
    here_kv, there_kv = halves(odd, narrow)
    at_keys, at_values = AT_KEYS * HEAD_SIZE, AT_VALUES * HEAD_SIZE
    copies = copied(
        [
            (v_ref.at[:, here_kv], vm),
            (v_ref.at[:, there_kv], vx),
            (q_ref.at[:, there], sent.at[:, :wide]),
            (g_ref.at[:, there], sent.at[:, wide : 2 * wide]),
            (k_ref.at[:, there_kv], sent.at[:, at_keys:at_values]),
            (v_ref.at[:, there_kv], sent.at[:, at_values:]),
            (q_ref.at[:, here], qm),
            (g_ref.at[:, here], gm),
        ],
        sem,
    )
    fill_bias(rank_ref[0], lens_ref, bias_ref)
    for copy in copies:
        copy.wait()


def order_kernel(rank_ref, mine, other, first, second):
    odd = rank_ref[0] % 2
    for core in range(CORES):

        @pl.when(odd == core)
        def _():
            (second if core else first)[...] = mine[...]
            (first if core else second)[...] = other[...]


def staged(units, *stages):
    held = {}
    for step in range(len(units) + len(stages) - 1):
        for depth, stage in enumerate(stages):
            at = step - depth
            if 0 <= at < len(units):
                held[at] = stage(*units[at], *held.get(at, ()))


UNITS = [(head, block) for head in range(CORE_HEADS) for block in range(CORES)]


def value_kernel(
    rank_ref, bias_ref, qm, gm, km, near, ka, kb,
    prob_ref, dvm, dvo,
):
    rows = qm.shape[0]
    odd = rank_ref[0] % 2 == 1
    grads = {}

    def score(head, block):
        blocks = (ka[:, span(head)], kb[:, span(head)]) + both(odd, km, near, head, AT_KEYS)
        queries = stacked(odd, qm, near, head, 0)[block]
        return (dot_last(jnp.concatenate(blocks[block : block + 3], axis=0), queries),)

    def normalise(head, block, scores):
        bias = jnp.concatenate([bias_ref[block]] * GROUP, axis=1)
        scores = scores * (score_scale * LOG2E) + bias
        top = jnp.max(scores, axis=0, keepdims=True)
        raised = jnp.exp2(scores - top)
        total = jnp.sum(raised, axis=0, keepdims=True)
        prob = (raised * (1.0 / total)).astype(jnp.bfloat16)
        prob_ref[head * CORES + block] = prob
        return (prob[: (2 - block) * rows],)

    def far_grads(head, block, prob):
        grads[block] = dot(prob, stacked(odd, gm, near, head, AT_GRADIENTS)[block])
        if block == 1:
            put(odd, dvm, dvo, head, grads[0][:rows], grads[0][rows:] + grads[1])
        return ()

    staged(UNITS, score, lambda head, block, scores: (scores,), normalise, far_grads)


def local_sum(core, pairs_ref, sources, head, rows):
    at = head * CORES + core
    total = dot(pairs_ref[at, 2 * rows :], sources[core])
    if core == 0:
        total += dot(pairs_ref[at + 1, rows : 2 * rows], sources[1])
    return total


def local_grads(core, prob_ref, dscore_ref, keys, values, queries, head, rows):
    at = head * CORES + core
    out = dot_first(prob_ref[at], jnp.concatenate(values[core : core + 3], axis=0))
    dq = dot_first(dscore_ref[at], jnp.concatenate(keys[core : core + 3], axis=0))
    dk = local_sum(core, dscore_ref, queries, head, rows)
    return out, dq, dk


def chosen(odd, pieces):
    return jnp.concatenate([jnp.where(odd, pieces[i], pieces[i + 1]) for i in range(3)], axis=0)


def other_sum(odd, pairs_ref, sources, head, rows):
    here = head * CORES
    mine = jnp.where(odd, sources[0], sources[1])
    total = dot(pairs_ref[here + jnp.where(odd, 0, 1), 2 * rows :], mine)
    return total + jnp.where(odd, dot(pairs_ref[here + 1, rows : 2 * rows], sources[1]), 0.0)


def key_kernel(
    rank_ref, prob_ref, qm, gm, vm, near, v2m, v2o,
    dscore_ref, dkm, dko,
):
    rows = qm.shape[0]
    odd = rank_ref[0] % 2 == 1
    grads = {}

    def value_blocks(head):
        return both(odd, v2m, v2o, head) + both(odd, vm, near, head, AT_VALUES)

    def product(head, block):
        gradients = stacked(odd, gm, near, head, AT_GRADIENTS)[block]
        values = jnp.concatenate(value_blocks(head)[block : block + 3], axis=0)
        return (dot_last(values, gradients),)

    def scale(head, block, dprob):
        at = head * CORES + block
        prob = prob_ref[at].astype(jnp.float32)
        delta = jnp.sum(prob * dprob, axis=0, keepdims=True)
        dscore = (prob * ((dprob - delta) * score_scale)).astype(jnp.bfloat16)
        dscore_ref[at] = dscore
        return (dscore[: (2 - block) * rows],)

    def far_grads(head, block, dscore):
        grads[block] = dot(dscore, stacked(odd, qm, near, head, 0)[block])
        if block == 1:
            put(odd, dkm, dko, head, grads[0][:rows], grads[0][rows:] + grads[1])
        return ()

    staged(UNITS, product, lambda head, block, dprob: (dprob,), scale, far_grads)


def sent_kernel(
    rank_ref, prob_ref, dscore_ref, qm, gm, km, vm, near, ka, kb, v2m, v2o,
    sent,
):
    rows = qm.shape[0]
    odd = rank_ref[0] % 2 == 1
    for head in range(CORE_HEADS):
        keys = (ka[:, span(head)], kb[:, span(head)]) + both(odd, km, near, head, AT_KEYS)
        at = head * CORES + jnp.where(odd, 0, 1)
        out = dot_first(prob_ref[at], chosen(odd, (both(odd, v2m, v2o, head) + both(odd, vm, near, head, AT_VALUES))))
        dq = dot_first(dscore_ref[at], chosen(odd, keys))
        for j in range(GROUP):
            piece = slice(j * rows, (j + 1) * rows)
            sent[:, span(head * GROUP + j)] = out[piece].astype(jnp.bfloat16)
            sent[:, span(AT_GRADIENTS + head * GROUP + j)] = dq[piece].astype(jnp.bfloat16)
        dk = other_sum(odd, dscore_ref, stacked(odd, qm, near, head, 0), head, rows)
        dv = other_sum(odd, prob_ref, stacked(odd, gm, near, head, AT_GRADIENTS), head, rows)
        sent[:, span(AT_KEYS + head)] = dk.astype(jnp.bfloat16)
        sent[:, span(AT_VALUES + head)] = dv.astype(jnp.bfloat16)


def own_kernel(
    rank_ref, prob_ref, dscore_ref, qm, gm, km, vm, near, ka, kb, v2m, v2o, backm,
    outm, dqm, dkm, dvm,
):
    rows = qm.shape[0]
    odd = rank_ref[0] % 2 == 1
    for core in range(CORES):

        @pl.when(rank_ref[0] % 2 == core)
        def _():
            for head in range(CORE_HEADS):
                keys = (ka[:, span(head)], kb[:, span(head)]) + both(odd, km, near, head, AT_KEYS)
                values = both(odd, v2m, v2o, head) + both(odd, vm, near, head, AT_VALUES)
                queries = stacked(odd, qm, near, head, 0)
                gradients = stacked(odd, gm, near, head, AT_GRADIENTS)
                out, dq, dk = local_grads(core, prob_ref, dscore_ref, keys, values, queries, head, rows)
                for j in range(GROUP):
                    at = slice(j * rows, (j + 1) * rows)
                    outm[:, span(head * GROUP + j)] = out[at].astype(jnp.bfloat16)
                    dqm[:, span(head * GROUP + j)] = dq[at]
                dkm[:, span(head)] = dk
                dv = local_sum(core, prob_ref, gradients, head, rows)
                dvm[:, span(head)] = dv + backm[:, span(head)].astype(jnp.float32)


def join_kernel(rank_ref, got, outm, dqm, dvm, backo, out_ref, dq_ref, dv_ref):
    odd = rank_ref[0] % CORES
    wide, narrow = outm.shape[1], dvm.shape[1]
    for core in range(CORES):
        here = slice(core * wide, (core + 1) * wide)
        there = slice((1 - core) * wide, (2 - core) * wide)

        @pl.when(odd == core)
        def _():
            out_ref[:, here] = outm[...]
            out_ref[:, there] = got[:, :wide]
            dq_ref[:, here] = dqm[...]
            dq_ref[:, there] = got[:, wide : 2 * wide].astype(jnp.float32)
            dv_ref[:, core * narrow : (core + 1) * narrow] = dvm[...]
            dv_ref[:, (1 - core) * narrow : (2 - core) * narrow] = backo[...].astype(jnp.float32) + got[
                :, AT_VALUES * HEAD_SIZE :
            ].astype(jnp.float32)


def add_kernel(offset, rank_ref, mine, near, backm, backo, target):
    odd = rank_ref[0] % 2
    width = mine.shape[1]
    offset = offset * HEAD_SIZE
    for core in range(CORES):
        here = slice(core * width, (core + 1) * width)
        there = slice((1 - core) * width, (2 - core) * width)

        @pl.when(odd == core)
        def _():
            target[:, here] = mine[...] + backm[...].astype(jnp.float32)
            target[:, there] = near[:, offset : offset + width].astype(jnp.float32) + backo[...].astype(jnp.float32)


def shape(dims, dtype):
    return jax.ShapeDtypeStruct(dims, dtype)


def run(kernel, name, outputs, index, *operands, far=(), scratch=()):
    small = pl.BlockSpec(memory_space=pltpu.SMEM)
    whole = pl.BlockSpec(memory_space=pltpu.VMEM)
    there = pl.BlockSpec(memory_space=pltpu.HBM)
    return pl.pallas_call(
        kernel,
        in_specs=[small] + [there if i in far else whole for i in range(len(operands))],
        out_specs=[whole] * len(outputs),
        out_shape=outputs,
        scratch_shapes=scratch,
        compiler_params=pltpu.CompilerParams(vmem_limit_bytes=40 * 2**20),
        cost_estimate=pl.CostEstimate(flops=COST.get(name, 0) * 1000000, bytes_accessed=1000, transcendentals=0),
        name=name,
    )(index, *operands)


def on_device(queries, keys, values, output_gradient, doc_lengths):
    rows = queries.shape[0]
    devices = lax.axis_size(AXES)
    index = lax.axis_index(AXES).reshape(1)
    docs = doc_lengths.shape[0]

    ahead = [(r, (r + 2) % devices) for r in range(devices)]
    across = [(r, ((r + 2) % devices) ^ 1) for r in range(devices)]
    behind = [(there, here) for here, there in ahead]
    recross = [(there, here) for here, there in across]
    swap = [(r, r ^ 1) for r in range(devices)]

    def moved(value, pairs):
        return lax.ppermute(value, AXES, pairs)

    narrow = shape((rows, keys.shape[1] // CORES), jnp.bfloat16)
    wide = shape((rows, queries.shape[1] // CORES), jnp.bfloat16)
    narrow_sum = shape(narrow.shape, jnp.float32)
    wide_sum = shape(wide.shape, jnp.float32)
    pairs = shape((KEY_VALUE_HEADS, 3 * rows, GROUP * rows), jnp.bfloat16)

    full = shape(keys.shape, jnp.float32)
    all_sent = shape((rows, ALL_SENT * HEAD_SIZE), jnp.bfloat16)
    def copies(count):
        return [pltpu.SemaphoreType.DMA((count,))]

    km, kx = run(split_kernel, "split_keys", [narrow] * 2, index, keys, far=(0,), scratch=copies(2))
    k2m, k2o = moved(km, ahead), moved(kx, across)
    queries, kx = lax.optimization_barrier((queries, kx))
    qm, gm, vm, vx, sent, bias = run(
        rows_kernel, "split_rows",
        [wide, wide, narrow, narrow, all_sent, shape((CORES, 3 * rows, rows), jnp.float32)],
        index, doc_lengths.reshape(1, docs), queries, output_gradient, keys, values,
        far=(1, 2, 3, 4), scratch=copies(8),
    )
    v2m, v2o = moved(vm, ahead), moved(vx, across)
    near = moved(sent, swap)
    ka, kb = run(order_kernel, "far_keys", [narrow] * 2, index, k2m, k2o)
    prob, dvm, dvo = run(
        value_kernel, "value_grads", [pairs, narrow, narrow],
        index, bias, qm, gm, km, near, ka, kb,
    )
    dvm, v2o = lax.optimization_barrier((dvm, v2o))
    dv_back = moved(dvm, behind), moved(dvo, recross)
    dscore, dkm, dko = run(
        key_kernel, "key_grads", [pairs, narrow, narrow],
        index, prob, qm, gm, vm, near, v2m, v2o,
    )
    dk_back = moved(dkm, behind), moved(dko, recross)
    prob, dv_back1 = lax.optimization_barrier((prob, dv_back[1]))
    dv_back = (dv_back[0], dv_back1)
    (sent,) = run(
        sent_kernel, "sent_grads", [all_sent],
        index, prob, dscore, qm, gm, km, vm, near, ka, kb, v2m, v2o,
    )
    got = moved(sent, swap)
    outm, dqm, dkm, dvm = run(
        own_kernel, "own_grads", [wide, wide_sum, narrow_sum, narrow_sum],
        index, prob, dscore, qm, gm, km, vm, near, ka, kb, v2m, v2o, dv_back[0],
    )
    got, dvm = lax.optimization_barrier((got, dvm))
    attended, dq, dv = run(
        join_kernel, "join_rows",
        [shape(queries.shape, jnp.bfloat16), shape(queries.shape, jnp.float32), full],
        index, got, outm, dqm, dvm, dv_back[1],
    )
    (dk,) = run(functools.partial(add_kernel, AT_KEYS), "join_keys", [full], index, dkm, got, *dk_back)
    return attended, dq, dk, dv


def solution(mesh):
    split = P(AXES, None)
    return jax.shard_map(
        on_device,
        mesh=mesh,
        in_specs=(split, split, split, split, P()),
        out_specs=(split, split, split, split),
        check_vma=False,
    )
```

```python
import functools

import jax
import jax.numpy as jnp
from jax import lax
from jax.experimental import pallas as pl
from jax.experimental.pallas import tpu as pltpu
from jax.sharding import PartitionSpec as P

QUERY_HEADS = 16
KEY_VALUE_HEADS = 8
HEAD_SIZE = 128
LOCAL_WINDOW = 256
GROUP = QUERY_HEADS // KEY_VALUE_HEADS
CORES = 2
CORE_HEADS = KEY_VALUE_HEADS // CORES
CORE_QUERIES = QUERY_HEADS // CORES
AT_GRADIENTS = CORE_QUERIES
AT_KEYS = 2 * CORE_QUERIES
AT_VALUES = AT_KEYS + CORE_HEADS
ALL_SENT = AT_VALUES + CORE_HEADS
AXES = ("dp", "seq")

score_scale = 168.0 ** (-0.5)
LOG2E = 1.4426950408889634
NEGATIVE = -1e30

CONTRACT_LAST = (((1,), (1,)), ((), ()))
CONTRACT_FIRST = (((0,), (0,)), ((), ()))


COST = {"own_grads": 20000, "split_keys": 20000, "far_keys": 20000}


def dot(a, b):
    return jnp.dot(a, b, preferred_element_type=jnp.float32)


def dot_last(a, b):
    return lax.dot_general(a, b, CONTRACT_LAST, preferred_element_type=jnp.float32)


def dot_first(a, b):
    return lax.dot_general(a, b, CONTRACT_FIRST, preferred_element_type=jnp.float32)


def span(head):
    return slice(head * HEAD_SIZE, (head + 1) * HEAD_SIZE)


def both(odd, mine, other, head, offset=0):
    a, b = mine[:, span(head)], other[:, span(offset + head)]
    return jnp.where(odd, b, a), jnp.where(odd, a, b)


def stacked(odd, mine, other, head, offset):
    pieces = [both(odd, mine, other, head * GROUP + j, offset) for j in range(GROUP)]
    return [jnp.concatenate([piece[block] for piece in pieces], axis=0) for block in range(CORES)]


def put(odd, mine, other, head, first, second, offset=0):
    mine[:, span(head)] = jnp.where(odd, second, first).astype(mine.dtype)
    other[:, span(offset + head)] = jnp.where(odd, first, second).astype(other.dtype)


def halves(odd, width):
    return (
        pl.ds(pl.multiple_of(odd * width, width), width),
        pl.ds(pl.multiple_of((1 - odd) * width, width), width),
    )


def copied(pairs, sem):
    copies = [pltpu.make_async_copy(source, target, sem.at[i]) for i, (source, target) in enumerate(pairs)]
    for copy in copies:
        copy.start()
    return copies


def split_kernel(rank_ref, source, mine, other, sem):
    here, there = halves(rank_ref[0] % CORES, mine.shape[1])
    for copy in copied([(source.at[:, here], mine), (source.at[:, there], other)], sem):
        copy.wait()


def fill_bias(rank, lens_ref, bias_ref):
    _, span_rows, rows = bias_ref.shape
    docs = lens_ref.shape[1]
    later = lax.broadcasted_iota(jnp.int32, (docs, docs), 0)
    earlier = lax.broadcasted_iota(jnp.int32, (docs, docs), 1)
    lens = jnp.broadcast_to(lens_ref[...].astype(jnp.float32), (docs, docs))
    ends = jnp.sum(jnp.where(earlier <= later, lens, 0.0), axis=1, keepdims=True)
    for block in range(CORES):
        first = (rank // CORES * CORES + block) * rows
        query = first + lax.broadcasted_iota(jnp.int32, (1, rows), 1)
        ended = jnp.where(ends <= query.astype(jnp.float32), ends, 0.0)
        start = jnp.max(ended, axis=0, keepdims=True).astype(jnp.int32)
        lowest = jnp.maximum(start, query - (LOCAL_WINDOW - 1))
        key = first - 2 * rows + lax.broadcasted_iota(jnp.int32, (span_rows, rows), 0)
        bias_ref[block] = jnp.where((key >= lowest) & (key <= query), 0.0, NEGATIVE)


def rows_kernel(
    rank_ref, lens_ref, q_ref, g_ref, k_ref, v_ref, qm, gm, vm, vx, sent, bias_ref, sem
):
    odd = rank_ref[0] % CORES
    wide, narrow = qm.shape[1], vm.shape[1]
    here, there = halves(odd, wide)
    here_kv, there_kv = halves(odd, narrow)
    at_keys, at_values = AT_KEYS * HEAD_SIZE, AT_VALUES * HEAD_SIZE
    copies = copied(
        [
            (v_ref.at[:, here_kv], vm),
            (v_ref.at[:, there_kv], vx),
            (q_ref.at[:, there], sent.at[:, :wide]),
            (g_ref.at[:, there], sent.at[:, wide : 2 * wide]),
            (k_ref.at[:, there_kv], sent.at[:, at_keys:at_values]),
            (v_ref.at[:, there_kv], sent.at[:, at_values:]),
            (q_ref.at[:, here], qm),
            (g_ref.at[:, here], gm),
        ],
        sem,
    )
    fill_bias(rank_ref[0], lens_ref, bias_ref)
    for copy in copies:
        copy.wait()


def order_kernel(rank_ref, mine, other, first, second):
    odd = rank_ref[0] % 2
    for core in range(CORES):

        @pl.when(odd == core)
        def _():
            (second if core else first)[...] = mine[...]
            (first if core else second)[...] = other[...]


def staged(units, *stages):
    held = {}
    for step in range(len(units) + len(stages) - 1):
        for depth, stage in enumerate(stages):
            at = step - depth
            if 0 <= at < len(units):
                held[at] = stage(*units[at], *held.get(at, ()))


UNITS = [(head, block) for head in range(CORE_HEADS) for block in range(CORES)]


def value_kernel(
    rank_ref, bias_ref, qm, gm, km, near, ka, kb,
    prob_ref, dvm, dvo,
):
    rows = qm.shape[0]
    odd = rank_ref[0] % 2 == 1
    grads = {}

    def score(head, block):
        blocks = (ka[:, span(head)], kb[:, span(head)]) + both(odd, km, near, head, AT_KEYS)
        queries = stacked(odd, qm, near, head, 0)[block]
        return (dot_last(jnp.concatenate(blocks[block : block + 3], axis=0), queries),)

    def normalise(head, block, scores):
        bias = jnp.concatenate([bias_ref[block]] * GROUP, axis=1)
        scores = scores * (score_scale * LOG2E) + bias
        top = jnp.max(scores, axis=0, keepdims=True)
        raised = jnp.exp2(scores - top)
        total = jnp.sum(raised, axis=0, keepdims=True)
        prob = (raised * (1.0 / total)).astype(jnp.bfloat16)
        prob_ref[head * CORES + block] = prob
        return (prob[: (2 - block) * rows],)

    def far_grads(head, block, prob):
        grads[block] = dot(prob, stacked(odd, gm, near, head, AT_GRADIENTS)[block])
        if block == 1:
            put(odd, dvm, dvo, head, grads[0][:rows], grads[0][rows:] + grads[1])
        return ()

    staged(UNITS, score, lambda head, block, scores: (scores,), normalise, far_grads)


def local_sum(core, pairs_ref, sources, head, rows):
    at = head * CORES + core
    total = dot(pairs_ref[at, 2 * rows :], sources[core])
    if core == 0:
        total += dot(pairs_ref[at + 1, rows : 2 * rows], sources[1])
    return total


def local_grads(core, prob_ref, dscore_ref, keys, values, queries, head, rows):
    at = head * CORES + core
    out = dot_first(prob_ref[at], jnp.concatenate(values[core : core + 3], axis=0))
    dq = dot_first(dscore_ref[at], jnp.concatenate(keys[core : core + 3], axis=0))
    dk = local_sum(core, dscore_ref, queries, head, rows)
    return out, dq, dk


def chosen(odd, pieces):
    return jnp.concatenate([jnp.where(odd, pieces[i], pieces[i + 1]) for i in range(3)], axis=0)


def other_sum(odd, pairs_ref, sources, head, rows):
    here = head * CORES
    mine = jnp.where(odd, sources[0], sources[1])
    total = dot(pairs_ref[here + jnp.where(odd, 0, 1), 2 * rows :], mine)
    return total + jnp.where(odd, dot(pairs_ref[here + 1, rows : 2 * rows], sources[1]), 0.0)


def key_kernel(
    rank_ref, prob_ref, qm, gm, vm, near, v2m, v2o,
    dscore_ref, dkm, dko,
):
    rows = qm.shape[0]
    odd = rank_ref[0] % 2 == 1
    grads = {}

    def value_blocks(head):
        return both(odd, v2m, v2o, head) + both(odd, vm, near, head, AT_VALUES)

    def product(head, block):
        gradients = stacked(odd, gm, near, head, AT_GRADIENTS)[block]
        values = jnp.concatenate(value_blocks(head)[block : block + 3], axis=0)
        return (dot_last(values, gradients),)

    def scale(head, block, dprob):
        at = head * CORES + block
        prob = prob_ref[at].astype(jnp.float32)
        delta = jnp.sum(prob * dprob, axis=0, keepdims=True)
        dscore = (prob * ((dprob - delta) * score_scale)).astype(jnp.bfloat16)
        dscore_ref[at] = dscore
        return (dscore[: (2 - block) * rows],)

    def far_grads(head, block, dscore):
        grads[block] = dot(dscore, stacked(odd, qm, near, head, 0)[block])
        if block == 1:
            put(odd, dkm, dko, head, grads[0][:rows], grads[0][rows:] + grads[1])
        return ()

    staged(UNITS, product, lambda head, block, dprob: (dprob,), scale, far_grads)


def sent_kernel(
    rank_ref, prob_ref, dscore_ref, qm, gm, km, vm, near, ka, kb, v2m, v2o,
    sent,
):
    rows = qm.shape[0]
    odd = rank_ref[0] % 2 == 1
    for head in range(CORE_HEADS):
        keys = (ka[:, span(head)], kb[:, span(head)]) + both(odd, km, near, head, AT_KEYS)
        at = head * CORES + jnp.where(odd, 0, 1)
        out = dot_first(prob_ref[at], chosen(odd, (both(odd, v2m, v2o, head) + both(odd, vm, near, head, AT_VALUES))))
        dq = dot_first(dscore_ref[at], chosen(odd, keys))
        for j in range(GROUP):
            piece = slice(j * rows, (j + 1) * rows)
            sent[:, span(head * GROUP + j)] = out[piece].astype(jnp.bfloat16)
            sent[:, span(AT_GRADIENTS + head * GROUP + j)] = dq[piece].astype(jnp.bfloat16)
        dk = other_sum(odd, dscore_ref, stacked(odd, qm, near, head, 0), head, rows)
        dv = other_sum(odd, prob_ref, stacked(odd, gm, near, head, AT_GRADIENTS), head, rows)
        sent[:, span(AT_KEYS + head)] = dk.astype(jnp.bfloat16)
        sent[:, span(AT_VALUES + head)] = dv.astype(jnp.bfloat16)


def own_kernel(
    rank_ref, prob_ref, dscore_ref, qm, gm, km, vm, near, ka, kb, v2m, v2o, backm,
    outm, dqm, dkm, dvm,
):
    rows = qm.shape[0]
    odd = rank_ref[0] % 2 == 1
    for core in range(CORES):

        @pl.when(rank_ref[0] % 2 == core)
        def _():
            for head in range(CORE_HEADS):
                keys = (ka[:, span(head)], kb[:, span(head)]) + both(odd, km, near, head, AT_KEYS)
                values = both(odd, v2m, v2o, head) + both(odd, vm, near, head, AT_VALUES)
                queries = stacked(odd, qm, near, head, 0)
                gradients = stacked(odd, gm, near, head, AT_GRADIENTS)
                out, dq, dk = local_grads(core, prob_ref, dscore_ref, keys, values, queries, head, rows)
                for j in range(GROUP):
                    at = slice(j * rows, (j + 1) * rows)
                    outm[:, span(head * GROUP + j)] = out[at].astype(jnp.bfloat16)
                    dqm[:, span(head * GROUP + j)] = dq[at]
                dkm[:, span(head)] = dk
                dv = local_sum(core, prob_ref, gradients, head, rows)
                dvm[:, span(head)] = dv + backm[:, span(head)].astype(jnp.float32)


def join_kernel(rank_ref, got, outm, dqm, dvm, backo, out_ref, dq_ref, dv_ref):
    odd = rank_ref[0] % CORES
    wide, narrow = outm.shape[1], dvm.shape[1]
    for core in range(CORES):
        here = slice(core * wide, (core + 1) * wide)
        there = slice((1 - core) * wide, (2 - core) * wide)

        @pl.when(odd == core)
        def _():
            out_ref[:, here] = outm[...]
            out_ref[:, there] = got[:, :wide]
            dq_ref[:, here] = dqm[...]
            dq_ref[:, there] = got[:, wide : 2 * wide].astype(jnp.float32)
            dv_ref[:, core * narrow : (core + 1) * narrow] = dvm[...]
            dv_ref[:, (1 - core) * narrow : (2 - core) * narrow] = backo[...].astype(jnp.float32) + got[
                :, AT_VALUES * HEAD_SIZE :
            ].astype(jnp.float32)


def add_kernel(offset, rank_ref, mine, near, backm, backo, target):
    odd = rank_ref[0] % 2
    width = mine.shape[1]
    offset = offset * HEAD_SIZE
    for core in range(CORES):
        here = slice(core * width, (core + 1) * width)
        there = slice((1 - core) * width, (2 - core) * width)

        @pl.when(odd == core)
        def _():
            target[:, here] = mine[...] + backm[...].astype(jnp.float32)
            target[:, there] = near[:, offset : offset + width].astype(jnp.float32) + backo[...].astype(jnp.float32)


def shape(dims, dtype):
    return jax.ShapeDtypeStruct(dims, dtype)


def run(kernel, name, outputs, index, *operands, far=(), scratch=()):
    small = pl.BlockSpec(memory_space=pltpu.SMEM)
    whole = pl.BlockSpec(memory_space=pltpu.VMEM)
    there = pl.BlockSpec(memory_space=pltpu.HBM)
    return pl.pallas_call(
        kernel,
        in_specs=[small] + [there if i in far else whole for i in range(len(operands))],
        out_specs=[whole] * len(outputs),
        out_shape=outputs,
        scratch_shapes=scratch,
        compiler_params=pltpu.CompilerParams(vmem_limit_bytes=40 * 2**20),
        cost_estimate=pl.CostEstimate(flops=COST.get(name, 0) * 1000000, bytes_accessed=1000, transcendentals=0),
        name=name,
    )(index, *operands)


def on_device(queries, keys, values, output_gradient, doc_lengths):
    rows = queries.shape[0]
    devices = lax.axis_size(AXES)
    index = lax.axis_index(AXES).reshape(1)
    docs = doc_lengths.shape[0]

    ahead = [(r, (r + 2) % devices) for r in range(devices)]
    across = [(r, ((r + 2) % devices) ^ 1) for r in range(devices)]
    behind = [(there, here) for here, there in ahead]
    recross = [(there, here) for here, there in across]
    swap = [(r, r ^ 1) for r in range(devices)]

    def moved(value, pairs):
        return lax.ppermute(value, AXES, pairs)

    narrow = shape((rows, keys.shape[1] // CORES), jnp.bfloat16)
    wide = shape((rows, queries.shape[1] // CORES), jnp.bfloat16)
    narrow_sum = shape(narrow.shape, jnp.float32)
    wide_sum = shape(wide.shape, jnp.float32)
    pairs = shape((KEY_VALUE_HEADS, 3 * rows, GROUP * rows), jnp.bfloat16)

    full = shape(keys.shape, jnp.float32)
    all_sent = shape((rows, ALL_SENT * HEAD_SIZE), jnp.bfloat16)
    def copies(count):
        return [pltpu.SemaphoreType.DMA((count,))]

    km, kx = run(split_kernel, "split_keys", [narrow] * 2, index, keys, far=(0,), scratch=copies(2))
    k2m, k2o = moved(km, ahead), moved(kx, across)
    queries, kx = lax.optimization_barrier((queries, kx))
    qm, gm, vm, vx, sent, bias = run(
        rows_kernel, "split_rows",
        [wide, wide, narrow, narrow, all_sent, shape((CORES, 3 * rows, rows), jnp.float32)],
        index, doc_lengths.reshape(1, docs), queries, output_gradient, keys, values,
        far=(1, 2, 3, 4), scratch=copies(8),
    )
    v2m, v2o = moved(vm, ahead), moved(vx, across)
    near = moved(sent, swap)
    ka, kb = run(order_kernel, "far_keys", [narrow] * 2, index, k2m, k2o)
    prob, dvm, dvo = run(
        value_kernel, "value_grads", [pairs, narrow, narrow],
        index, bias, qm, gm, km, near, ka, kb,
    )
    dvo, v2o = lax.optimization_barrier((dvo, v2o))
    dv_back = moved(dvm, behind), moved(dvo, recross)
    dscore, dkm, dko = run(
        key_kernel, "key_grads", [pairs, narrow, narrow],
        index, prob, qm, gm, vm, near, v2m, v2o,
    )
    dk_back = moved(dkm, behind), moved(dko, recross)
    prob, dv_back1 = lax.optimization_barrier((prob, dv_back[1]))
    dv_back = (dv_back[0], dv_back1)
    (sent,) = run(
        sent_kernel, "sent_grads", [all_sent],
        index, prob, dscore, qm, gm, km, vm, near, ka, kb, v2m, v2o,
    )
    got = moved(sent, swap)
    outm, dqm, dkm, dvm = run(
        own_kernel, "own_grads", [wide, wide_sum, narrow_sum, narrow_sum],
        index, prob, dscore, qm, gm, km, vm, near, ka, kb, v2m, v2o, dv_back[0],
    )
    got, dvm = lax.optimization_barrier((got, dvm))
    attended, dq, dv = run(
        join_kernel, "join_rows",
        [shape(queries.shape, jnp.bfloat16), shape(queries.shape, jnp.float32), full],
        index, got, outm, dqm, dvm, dv_back[1],
    )
    (dk,) = run(functools.partial(add_kernel, AT_KEYS), "join_keys", [full], index, dkm, got, *dk_back)
    return attended, dq, dk, dv


def solution(mesh):
    split = P(AXES, None)
    return jax.shard_map(
        on_device,
        mesh=mesh,
        in_specs=(split, split, split, split, P()),
        out_specs=(split, split, split, split),
        check_vma=False,
    )
```

```python
import functools

import jax
import jax.numpy as jnp
from jax import lax
from jax.experimental import pallas as pl
from jax.experimental.pallas import tpu as pltpu
from jax.sharding import PartitionSpec as P

QUERY_HEADS = 16
KEY_VALUE_HEADS = 8
HEAD_SIZE = 128
LOCAL_WINDOW = 256
GROUP = QUERY_HEADS // KEY_VALUE_HEADS
CORES = 2
CORE_HEADS = KEY_VALUE_HEADS // CORES
CORE_QUERIES = QUERY_HEADS // CORES
AT_GRADIENTS = CORE_QUERIES
AT_KEYS = 2 * CORE_QUERIES
AT_VALUES = AT_KEYS + CORE_HEADS
ALL_SENT = AT_VALUES + CORE_HEADS
AXES = ("dp", "seq")

score_scale = 168.0 ** (-0.5)
LOG2E = 1.4426950408889634
NEGATIVE = -1e30

CONTRACT_LAST = (((1,), (1,)), ((), ()))
CONTRACT_FIRST = (((0,), (0,)), ((), ()))


COST = {"own_grads": 20000, "split_keys": 20000, "far_keys": 20000}


def dot(a, b):
    return jnp.dot(a, b, preferred_element_type=jnp.float32)


def dot_last(a, b):
    return lax.dot_general(a, b, CONTRACT_LAST, preferred_element_type=jnp.float32)


def dot_first(a, b):
    return lax.dot_general(a, b, CONTRACT_FIRST, preferred_element_type=jnp.float32)


def span(head):
    return slice(head * HEAD_SIZE, (head + 1) * HEAD_SIZE)


def both(odd, mine, other, head, offset=0):
    a, b = mine[:, span(head)], other[:, span(offset + head)]
    return jnp.where(odd, b, a), jnp.where(odd, a, b)


def stacked(odd, mine, other, head, offset):
    pieces = [both(odd, mine, other, head * GROUP + j, offset) for j in range(GROUP)]
    return [jnp.concatenate([piece[block] for piece in pieces], axis=0) for block in range(CORES)]


def put(odd, mine, other, head, first, second, offset=0):
    mine[:, span(head)] = jnp.where(odd, second, first).astype(mine.dtype)
    other[:, span(offset + head)] = jnp.where(odd, first, second).astype(other.dtype)


def halves(odd, width):
    return (
        pl.ds(pl.multiple_of(odd * width, width), width),
        pl.ds(pl.multiple_of((1 - odd) * width, width), width),
    )


def copied(pairs, sem):
    copies = [pltpu.make_async_copy(source, target, sem.at[i]) for i, (source, target) in enumerate(pairs)]
    for copy in copies:
        copy.start()
    return copies


def split_kernel(rank_ref, source, mine, other, sem):
    here, there = halves(rank_ref[0] % CORES, mine.shape[1])
    for copy in copied([(source.at[:, here], mine), (source.at[:, there], other)], sem):
        copy.wait()


def fill_bias(rank, lens_ref, bias_ref):
    _, span_rows, rows = bias_ref.shape
    docs = lens_ref.shape[1]
    later = lax.broadcasted_iota(jnp.int32, (docs, docs), 0)
    earlier = lax.broadcasted_iota(jnp.int32, (docs, docs), 1)
    lens = jnp.broadcast_to(lens_ref[...].astype(jnp.float32), (docs, docs))
    ends = jnp.sum(jnp.where(earlier <= later, lens, 0.0), axis=1, keepdims=True)
    for block in range(CORES):
        first = (rank // CORES * CORES + block) * rows
        query = first + lax.broadcasted_iota(jnp.int32, (1, rows), 1)
        ended = jnp.where(ends <= query.astype(jnp.float32), ends, 0.0)
        start = jnp.max(ended, axis=0, keepdims=True).astype(jnp.int32)
        lowest = jnp.maximum(start, query - (LOCAL_WINDOW - 1))
        key = first - 2 * rows + lax.broadcasted_iota(jnp.int32, (span_rows, rows), 0)
        bias_ref[block] = jnp.where((key >= lowest) & (key <= query), 0.0, NEGATIVE)


def rows_kernel(
    rank_ref, lens_ref, q_ref, g_ref, k_ref, v_ref, qm, gm, vm, vx, sent, bias_ref, sem
):
    odd = rank_ref[0] % CORES
    wide, narrow = qm.shape[1], vm.shape[1]
    here, there = halves(odd, wide)
    here_kv, there_kv = halves(odd, narrow)
    at_keys, at_values = AT_KEYS * HEAD_SIZE, AT_VALUES * HEAD_SIZE
    copies = copied(
        [
            (v_ref.at[:, here_kv], vm),
            (v_ref.at[:, there_kv], vx),
            (q_ref.at[:, there], sent.at[:, :wide]),
            (g_ref.at[:, there], sent.at[:, wide : 2 * wide]),
            (k_ref.at[:, there_kv], sent.at[:, at_keys:at_values]),
            (v_ref.at[:, there_kv], sent.at[:, at_values:]),
            (q_ref.at[:, here], qm),
            (g_ref.at[:, here], gm),
        ],
        sem,
    )
    fill_bias(rank_ref[0], lens_ref, bias_ref)
    for copy in copies:
        copy.wait()


def mark_kernel(rank_ref, source, target):
    target[...] = source[: target.shape[0], : target.shape[1]]


def order_kernel(rank_ref, mine, other, mark, first, second):
    odd = rank_ref[0] % 2
    for core in range(CORES):

        @pl.when(odd == core)
        def _():
            (second if core else first)[...] = mine[...]
            (first if core else second)[...] = other[...]


def staged(units, *stages):
    held = {}
    for step in range(len(units) + len(stages) - 1):
        for depth, stage in enumerate(stages):
            at = step - depth
            if 0 <= at < len(units):
                held[at] = stage(*units[at], *held.get(at, ()))


UNITS = [(head, block) for head in range(CORE_HEADS) for block in range(CORES)]


def value_kernel(
    rank_ref, bias_ref, qm, gm, km, near, ka, kb,
    prob_ref, dvm, dvo,
):
    rows = qm.shape[0]
    odd = rank_ref[0] % 2 == 1
    grads = {}

    def score(head, block):
        blocks = (ka[:, span(head)], kb[:, span(head)]) + both(odd, km, near, head, AT_KEYS)
        queries = stacked(odd, qm, near, head, 0)[block]
        return (dot_last(jnp.concatenate(blocks[block : block + 3], axis=0), queries),)

    def normalise(head, block, scores):
        bias = jnp.concatenate([bias_ref[block]] * GROUP, axis=1)
        scores = scores * (score_scale * LOG2E) + bias
        top = jnp.max(scores, axis=0, keepdims=True)
        raised = jnp.exp2(scores - top)
        total = jnp.sum(raised, axis=0, keepdims=True)
        prob = (raised * (1.0 / total)).astype(jnp.bfloat16)
        prob_ref[head * CORES + block] = prob
        return (prob[: (2 - block) * rows],)

    def far_grads(head, block, prob):
        grads[block] = dot(prob, stacked(odd, gm, near, head, AT_GRADIENTS)[block])
        if block == 1:
            put(odd, dvm, dvo, head, grads[0][:rows], grads[0][rows:] + grads[1])
        return ()

    staged(UNITS, score, lambda head, block, scores: (scores,), normalise, far_grads)


def local_sum(core, pairs_ref, sources, head, rows):
    at = head * CORES + core
    total = dot(pairs_ref[at, 2 * rows :], sources[core])
    if core == 0:
        total += dot(pairs_ref[at + 1, rows : 2 * rows], sources[1])
    return total


def local_grads(core, prob_ref, dscore_ref, keys, values, queries, head, rows):
    at = head * CORES + core
    out = dot_first(prob_ref[at], jnp.concatenate(values[core : core + 3], axis=0))
    dq = dot_first(dscore_ref[at], jnp.concatenate(keys[core : core + 3], axis=0))
    dk = local_sum(core, dscore_ref, queries, head, rows)
    return out, dq, dk


def chosen(odd, pieces):
    return jnp.concatenate([jnp.where(odd, pieces[i], pieces[i + 1]) for i in range(3)], axis=0)


def other_sum(odd, pairs_ref, sources, head, rows):
    here = head * CORES
    mine = jnp.where(odd, sources[0], sources[1])
    total = dot(pairs_ref[here + jnp.where(odd, 0, 1), 2 * rows :], mine)
    return total + jnp.where(odd, dot(pairs_ref[here + 1, rows : 2 * rows], sources[1]), 0.0)


def near_kernel(rank_ref, gm, vm, near, dprob_ref):
    rows = gm.shape[0]
    odd = rank_ref[0] % 2 == 1
    for head, block in UNITS:
        values = jnp.concatenate(both(odd, vm, near, head, AT_VALUES)[: block + 1], axis=0)
        gradients = stacked(odd, gm, near, head, AT_GRADIENTS)[block]
        dprob_ref[head * CORES + block, : (block + 1) * rows] = dot_last(values, gradients)


def key_kernel(
    rank_ref, near_dprob, prob_ref, qm, gm, vm, near, v2m, v2o,
    dscore_ref, dkm, dko,
):
    rows = qm.shape[0]
    odd = rank_ref[0] % 2 == 1
    grads = {}

    def value_blocks(head):
        return both(odd, v2m, v2o, head) + both(odd, vm, near, head, AT_VALUES)

    def product(head, block):
        gradients = stacked(odd, gm, near, head, AT_GRADIENTS)[block]
        values = jnp.concatenate(both(odd, v2m, v2o, head)[block:], axis=0)
        far = dot_last(values, gradients)
        return (jnp.concatenate([far, near_dprob[head * CORES + block, : (block + 1) * rows]], axis=0),)

    def scale(head, block, dprob):
        at = head * CORES + block
        prob = prob_ref[at].astype(jnp.float32)
        delta = jnp.sum(prob * dprob, axis=0, keepdims=True)
        dscore = (prob * ((dprob - delta) * score_scale)).astype(jnp.bfloat16)
        dscore_ref[at] = dscore
        return (dscore[: (2 - block) * rows],)

    def far_grads(head, block, dscore):
        grads[block] = dot(dscore, stacked(odd, qm, near, head, 0)[block])
        if block == 1:
            put(odd, dkm, dko, head, grads[0][:rows], grads[0][rows:] + grads[1])
        return ()

    staged(UNITS, product, lambda head, block, dprob: (dprob,), scale, far_grads)


def sent_kernel(
    rank_ref, prob_ref, dscore_ref, qm, gm, km, vm, near, ka, kb, v2m, v2o,
    sent,
):
    rows = qm.shape[0]
    odd = rank_ref[0] % 2 == 1
    for head in range(CORE_HEADS):
        keys = (ka[:, span(head)], kb[:, span(head)]) + both(odd, km, near, head, AT_KEYS)
        at = head * CORES + jnp.where(odd, 0, 1)
        out = dot_first(prob_ref[at], chosen(odd, (both(odd, v2m, v2o, head) + both(odd, vm, near, head, AT_VALUES))))
        dq = dot_first(dscore_ref[at], chosen(odd, keys))
        for j in range(GROUP):
            piece = slice(j * rows, (j + 1) * rows)
            sent[:, span(head * GROUP + j)] = out[piece].astype(jnp.bfloat16)
            sent[:, span(AT_GRADIENTS + head * GROUP + j)] = dq[piece].astype(jnp.bfloat16)
        dk = other_sum(odd, dscore_ref, stacked(odd, qm, near, head, 0), head, rows)
        dv = other_sum(odd, prob_ref, stacked(odd, gm, near, head, AT_GRADIENTS), head, rows)
        sent[:, span(AT_KEYS + head)] = dk.astype(jnp.bfloat16)
        sent[:, span(AT_VALUES + head)] = dv.astype(jnp.bfloat16)


def own_kernel(
    rank_ref, prob_ref, dscore_ref, qm, gm, km, vm, near, ka, kb, v2m, v2o, backm,
    outm, dqm, dkm, dvm,
):
    rows = qm.shape[0]
    odd = rank_ref[0] % 2 == 1
    for core in range(CORES):

        @pl.when(rank_ref[0] % 2 == core)
        def _():
            for head in range(CORE_HEADS):
                keys = (ka[:, span(head)], kb[:, span(head)]) + both(odd, km, near, head, AT_KEYS)
                values = both(odd, v2m, v2o, head) + both(odd, vm, near, head, AT_VALUES)
                queries = stacked(odd, qm, near, head, 0)
                gradients = stacked(odd, gm, near, head, AT_GRADIENTS)
                out, dq, dk = local_grads(core, prob_ref, dscore_ref, keys, values, queries, head, rows)
                for j in range(GROUP):
                    at = slice(j * rows, (j + 1) * rows)
                    outm[:, span(head * GROUP + j)] = out[at].astype(jnp.bfloat16)
                    dqm[:, span(head * GROUP + j)] = dq[at]
                dkm[:, span(head)] = dk
                dv = local_sum(core, prob_ref, gradients, head, rows)
                dvm[:, span(head)] = dv + backm[:, span(head)].astype(jnp.float32)


def join_kernel(rank_ref, got, outm, dqm, dvm, backo, out_ref, dq_ref, dv_ref):
    odd = rank_ref[0] % CORES
    wide, narrow = outm.shape[1], dvm.shape[1]
    for core in range(CORES):
        here = slice(core * wide, (core + 1) * wide)
        there = slice((1 - core) * wide, (2 - core) * wide)

        @pl.when(odd == core)
        def _():
            out_ref[:, here] = outm[...]
            out_ref[:, there] = got[:, :wide]
            dq_ref[:, here] = dqm[...]
            dq_ref[:, there] = got[:, wide : 2 * wide].astype(jnp.float32)
            dv_ref[:, core * narrow : (core + 1) * narrow] = dvm[...]
            dv_ref[:, (1 - core) * narrow : (2 - core) * narrow] = backo[...].astype(jnp.float32) + got[
                :, AT_VALUES * HEAD_SIZE :
            ].astype(jnp.float32)


def add_kernel(offset, rank_ref, mine, near, backm, backo, target):
    odd = rank_ref[0] % 2
    width = mine.shape[1]
    offset = offset * HEAD_SIZE
    for core in range(CORES):
        here = slice(core * width, (core + 1) * width)
        there = slice((1 - core) * width, (2 - core) * width)

        @pl.when(odd == core)
        def _():
            target[:, here] = mine[...] + backm[...].astype(jnp.float32)
            target[:, there] = near[:, offset : offset + width].astype(jnp.float32) + backo[...].astype(jnp.float32)


def shape(dims, dtype):
    return jax.ShapeDtypeStruct(dims, dtype)


def run(kernel, name, outputs, index, *operands, far=(), scratch=()):
    small = pl.BlockSpec(memory_space=pltpu.SMEM)
    whole = pl.BlockSpec(memory_space=pltpu.VMEM)
    there = pl.BlockSpec(memory_space=pltpu.HBM)
    return pl.pallas_call(
        kernel,
        in_specs=[small] + [there if i in far else whole for i in range(len(operands))],
        out_specs=[whole] * len(outputs),
        out_shape=outputs,
        scratch_shapes=scratch,
        compiler_params=pltpu.CompilerParams(vmem_limit_bytes=40 * 2**20),
        cost_estimate=pl.CostEstimate(flops=COST.get(name, 0) * 1000000, bytes_accessed=1000, transcendentals=0),
        name=name,
    )(index, *operands)


def on_device(queries, keys, values, output_gradient, doc_lengths):
    rows = queries.shape[0]
    devices = lax.axis_size(AXES)
    index = lax.axis_index(AXES).reshape(1)
    docs = doc_lengths.shape[0]

    ahead = [(r, (r + 2) % devices) for r in range(devices)]
    across = [(r, ((r + 2) % devices) ^ 1) for r in range(devices)]
    behind = [(there, here) for here, there in ahead]
    recross = [(there, here) for here, there in across]
    swap = [(r, r ^ 1) for r in range(devices)]

    def moved(value, pairs):
        return lax.ppermute(value, AXES, pairs)

    narrow = shape((rows, keys.shape[1] // CORES), jnp.bfloat16)
    wide = shape((rows, queries.shape[1] // CORES), jnp.bfloat16)
    narrow_sum = shape(narrow.shape, jnp.float32)
    wide_sum = shape(wide.shape, jnp.float32)
    pairs = shape((KEY_VALUE_HEADS, 3 * rows, GROUP * rows), jnp.bfloat16)

    full = shape(keys.shape, jnp.float32)
    all_sent = shape((rows, ALL_SENT * HEAD_SIZE), jnp.bfloat16)
    def copies(count):
        return [pltpu.SemaphoreType.DMA((count,))]

    km, kx = run(split_kernel, "split_keys", [narrow] * 2, index, keys, far=(0,), scratch=copies(2))
    k2m, k2o = moved(km, ahead), moved(kx, across)
    queries, kx = lax.optimization_barrier((queries, kx))
    qm, gm, vm, vx, sent, bias = run(
        rows_kernel, "split_rows",
        [wide, wide, narrow, narrow, all_sent, shape((CORES, 3 * rows, rows), jnp.float32)],
        index, doc_lengths.reshape(1, docs), queries, output_gradient, keys, values,
        far=(1, 2, 3, 4), scratch=copies(8),
    )
    v2m, v2o = moved(vm, ahead), moved(vx, across)
    near = moved(sent, swap)
    (mark,) = run(mark_kernel, "mark", [shape((16, HEAD_SIZE), jnp.bfloat16)], index, k2m)
    ka, kb = run(order_kernel, "far_keys", [narrow] * 2, index, k2m, k2o, mark)
    prob, dvm, dvo = run(
        value_kernel, "value_grads", [pairs, narrow, narrow],
        index, bias, qm, gm, km, near, ka, kb,
    )
    later_rows, dvm, dvo = lax.optimization_barrier((gm, dvm, dvo))
    (near_dprob,) = run(
        near_kernel, "near_values", [shape((KEY_VALUE_HEADS, 2 * rows, GROUP * rows), jnp.float32)],
        index, later_rows, vm, near,
    )
    dvo, v2o, near_dprob = lax.optimization_barrier((dvo, v2o, near_dprob))
    dv_back = moved(dvm, behind), moved(dvo, recross)
    dscore, dkm, dko = run(
        key_kernel, "key_grads", [pairs, narrow, narrow],
        index, near_dprob, prob, qm, gm, vm, near, v2m, v2o,
    )
    dk_back = moved(dkm, behind), moved(dko, recross)
    prob, dv_back1 = lax.optimization_barrier((prob, dv_back[1]))
    dv_back = (dv_back[0], dv_back1)
    (sent,) = run(
        sent_kernel, "sent_grads", [all_sent],
        index, prob, dscore, qm, gm, km, vm, near, ka, kb, v2m, v2o,
    )
    got = moved(sent, swap)
    outm, dqm, dkm, dvm = run(
        own_kernel, "own_grads", [wide, wide_sum, narrow_sum, narrow_sum],
        index, prob, dscore, qm, gm, km, vm, near, ka, kb, v2m, v2o, dv_back[0],
    )
    got, dvm = lax.optimization_barrier((got, dvm))
    attended, dq, dv = run(
        join_kernel, "join_rows",
        [shape(queries.shape, jnp.bfloat16), shape(queries.shape, jnp.float32), full],
        index, got, outm, dqm, dvm, dv_back[1],
    )
    (dk,) = run(functools.partial(add_kernel, AT_KEYS), "join_keys", [full], index, dkm, got, *dk_back)
    return attended, dq, dk, dv


def solution(mesh):
    split = P(AXES, None)
    return jax.shard_map(
        on_device,
        mesh=mesh,
        in_specs=(split, split, split, split, P()),
        out_specs=(split, split, split, split),
        check_vma=False,
    )
```

```python
import functools

import jax
import jax.numpy as jnp
from jax import lax
from jax.experimental import pallas as pl
from jax.experimental.pallas import tpu as pltpu
from jax.sharding import PartitionSpec as P

QUERY_HEADS = 16
KEY_VALUE_HEADS = 8
HEAD_SIZE = 128
LOCAL_WINDOW = 256
GROUP = QUERY_HEADS // KEY_VALUE_HEADS
CORES = 2
CORE_HEADS = KEY_VALUE_HEADS // CORES
CORE_QUERIES = QUERY_HEADS // CORES
AT_GRADIENTS = CORE_QUERIES
AT_KEYS = 2 * CORE_QUERIES
AT_VALUES = AT_KEYS + CORE_HEADS
ALL_SENT = AT_VALUES + CORE_HEADS
AXES = ("dp", "seq")

score_scale = 168.0 ** (-0.5)
LOG2E = 1.4426950408889634
NEGATIVE = -1e30

CONTRACT_LAST = (((1,), (1,)), ((), ()))
CONTRACT_FIRST = (((0,), (0,)), ((), ()))


COST = {"own_grads": 20000, "split_keys": 20000, "far_keys": 20000}


def dot(a, b):
    return jnp.dot(a, b, preferred_element_type=jnp.float32)


def dot_last(a, b):
    return lax.dot_general(a, b, CONTRACT_LAST, preferred_element_type=jnp.float32)


def dot_first(a, b):
    return lax.dot_general(a, b, CONTRACT_FIRST, preferred_element_type=jnp.float32)


def span(head):
    return slice(head * HEAD_SIZE, (head + 1) * HEAD_SIZE)


def both(odd, mine, other, head, offset=0):
    a, b = mine[:, span(head)], other[:, span(offset + head)]
    return jnp.where(odd, b, a), jnp.where(odd, a, b)


def stacked(odd, mine, other, head, offset):
    pieces = [both(odd, mine, other, head * GROUP + j, offset) for j in range(GROUP)]
    return [jnp.concatenate([piece[block] for piece in pieces], axis=0) for block in range(CORES)]


def put(odd, mine, other, head, first, second, offset=0):
    mine[:, span(head)] = jnp.where(odd, second, first).astype(mine.dtype)
    other[:, span(offset + head)] = jnp.where(odd, first, second).astype(other.dtype)


def halves(odd, width):
    return (
        pl.ds(pl.multiple_of(odd * width, width), width),
        pl.ds(pl.multiple_of((1 - odd) * width, width), width),
    )


def copied(pairs, sem):
    copies = [pltpu.make_async_copy(source, target, sem.at[i]) for i, (source, target) in enumerate(pairs)]
    for copy in copies:
        copy.start()
    return copies


def split_kernel(rank_ref, source, mine, other, sem):
    here, there = halves(rank_ref[0] % CORES, mine.shape[1])
    for copy in copied([(source.at[:, here], mine), (source.at[:, there], other)], sem):
        copy.wait()


def fill_bias(rank, lens_ref, bias_ref):
    _, span_rows, rows = bias_ref.shape
    docs = lens_ref.shape[1]
    later = lax.broadcasted_iota(jnp.int32, (docs, docs), 0)
    earlier = lax.broadcasted_iota(jnp.int32, (docs, docs), 1)
    lens = jnp.broadcast_to(lens_ref[...].astype(jnp.float32), (docs, docs))
    ends = jnp.sum(jnp.where(earlier <= later, lens, 0.0), axis=1, keepdims=True)
    for block in range(CORES):
        first = (rank // CORES * CORES + block) * rows
        query = first + lax.broadcasted_iota(jnp.int32, (1, rows), 1)
        ended = jnp.where(ends <= query.astype(jnp.float32), ends, 0.0)
        start = jnp.max(ended, axis=0, keepdims=True).astype(jnp.int32)
        lowest = jnp.maximum(start, query - (LOCAL_WINDOW - 1))
        key = first - 2 * rows + lax.broadcasted_iota(jnp.int32, (span_rows, rows), 0)
        bias_ref[block] = jnp.where((key >= lowest) & (key <= query), 0.0, NEGATIVE)


def rows_kernel(
    rank_ref, lens_ref, q_ref, g_ref, k_ref, v_ref, qm, gm, vm, vx, sent, bias_ref, sem
):
    odd = rank_ref[0] % CORES
    wide, narrow = qm.shape[1], vm.shape[1]
    here, there = halves(odd, wide)
    here_kv, there_kv = halves(odd, narrow)
    at_keys, at_values = AT_KEYS * HEAD_SIZE, AT_VALUES * HEAD_SIZE
    copies = copied(
        [
            (v_ref.at[:, here_kv], vm),
            (v_ref.at[:, there_kv], vx),
            (q_ref.at[:, there], sent.at[:, :wide]),
            (g_ref.at[:, there], sent.at[:, wide : 2 * wide]),
            (k_ref.at[:, there_kv], sent.at[:, at_keys:at_values]),
            (v_ref.at[:, there_kv], sent.at[:, at_values:]),
            (q_ref.at[:, here], qm),
            (g_ref.at[:, here], gm),
        ],
        sem,
    )
    fill_bias(rank_ref[0], lens_ref, bias_ref)
    for copy in copies:
        copy.wait()


def mark_kernel(rank_ref, source, target):
    target[...] = source[: target.shape[0], : target.shape[1]]


def order_kernel(rank_ref, mine, other, mark, first, second):
    odd = rank_ref[0] % 2
    for core in range(CORES):

        @pl.when(odd == core)
        def _():
            (second if core else first)[...] = mine[...]
            (first if core else second)[...] = other[...]


def staged(units, *stages):
    held = {}
    for step in range(len(units) + len(stages) - 1):
        for depth, stage in enumerate(stages):
            at = step - depth
            if 0 <= at < len(units):
                held[at] = stage(*units[at], *held.get(at, ()))


UNITS = [(head, block) for head in range(CORE_HEADS) for block in range(CORES)]


def value_kernel(
    rank_ref, bias_ref, qm, gm, km, near, ka, kb,
    prob_ref, dvm, dvo,
):
    rows = qm.shape[0]
    odd = rank_ref[0] % 2 == 1
    grads = {}

    def score(head, block):
        blocks = (ka[:, span(head)], kb[:, span(head)]) + both(odd, km, near, head, AT_KEYS)
        queries = stacked(odd, qm, near, head, 0)[block]
        return (dot_last(jnp.concatenate(blocks[block : block + 3], axis=0), queries),)

    def normalise(head, block, scores):
        bias = jnp.concatenate([bias_ref[block]] * GROUP, axis=1)
        scores = scores * (score_scale * LOG2E) + bias
        top = jnp.max(scores, axis=0, keepdims=True)
        raised = jnp.exp2(scores - top)
        total = jnp.sum(raised, axis=0, keepdims=True)
        prob = (raised * (1.0 / total)).astype(jnp.bfloat16)
        prob_ref[head * CORES + block] = prob
        return (prob[: (2 - block) * rows],)

    def far_grads(head, block, prob):
        grads[block] = dot(prob, stacked(odd, gm, near, head, AT_GRADIENTS)[block])
        if block == 1:
            put(odd, dvm, dvo, head, grads[0][:rows], grads[0][rows:] + grads[1])
        return ()

    staged(UNITS, score, lambda head, block, scores: (scores,), normalise, far_grads)


def local_sum(core, pairs_ref, sources, head, rows):
    at = head * CORES + core
    total = dot(pairs_ref[at, 2 * rows :], sources[core])
    if core == 0:
        total += dot(pairs_ref[at + 1, rows : 2 * rows], sources[1])
    return total


def local_grads(core, prob_ref, dscore_ref, keys, values, queries, head, rows):
    at = head * CORES + core
    out = dot_first(prob_ref[at], jnp.concatenate(values[core : core + 3], axis=0))
    dq = dot_first(dscore_ref[at], jnp.concatenate(keys[core : core + 3], axis=0))
    dk = local_sum(core, dscore_ref, queries, head, rows)
    return out, dq, dk


def chosen(odd, pieces):
    return jnp.concatenate([jnp.where(odd, pieces[i], pieces[i + 1]) for i in range(3)], axis=0)


def other_sum(odd, pairs_ref, sources, head, rows):
    here = head * CORES
    mine = jnp.where(odd, sources[0], sources[1])
    total = dot(pairs_ref[here + jnp.where(odd, 0, 1), 2 * rows :], mine)
    return total + jnp.where(odd, dot(pairs_ref[here + 1, rows : 2 * rows], sources[1]), 0.0)


def near_kernel(rank_ref, gm, vm, near, dprob_ref):
    rows = gm.shape[0]
    odd = rank_ref[0] % 2 == 1
    for head, block in UNITS:
        values = jnp.concatenate(both(odd, vm, near, head, AT_VALUES)[: block + 1], axis=0)
        gradients = stacked(odd, gm, near, head, AT_GRADIENTS)[block]
        dprob_ref[head * CORES + block, : (block + 1) * rows] = dot_last(values, gradients)


def key_kernel(
    rank_ref, near_dprob, prob_ref, qm, gm, vm, near, v2m, v2o,
    dscore_ref, dkm, dko,
):
    rows = qm.shape[0]
    odd = rank_ref[0] % 2 == 1
    grads = {}

    def value_blocks(head):
        return both(odd, v2m, v2o, head) + both(odd, vm, near, head, AT_VALUES)

    def product(head, block):
        gradients = stacked(odd, gm, near, head, AT_GRADIENTS)[block]
        values = jnp.concatenate(both(odd, v2m, v2o, head)[block:], axis=0)
        far = dot_last(values, gradients)
        return (jnp.concatenate([far, near_dprob[head * CORES + block, : (block + 1) * rows]], axis=0),)

    def scale(head, block, dprob):
        at = head * CORES + block
        prob = prob_ref[at].astype(jnp.float32)
        delta = jnp.sum(prob * dprob, axis=0, keepdims=True)
        dscore = (prob * ((dprob - delta) * score_scale)).astype(jnp.bfloat16)
        dscore_ref[at] = dscore
        return (dscore[: (2 - block) * rows],)

    def far_grads(head, block, dscore):
        grads[block] = dot(dscore, stacked(odd, qm, near, head, 0)[block])
        if block == 1:
            put(odd, dkm, dko, head, grads[0][:rows], grads[0][rows:] + grads[1])
        return ()

    staged(UNITS, product, lambda head, block, dprob: (dprob,), scale, far_grads)


def sent_kernel(
    rank_ref, prob_ref, dscore_ref, qm, gm, km, vm, near, ka, kb, v2m, v2o,
    sent,
):
    rows = qm.shape[0]
    odd = rank_ref[0] % 2 == 1
    for head in range(CORE_HEADS):
        keys = (ka[:, span(head)], kb[:, span(head)]) + both(odd, km, near, head, AT_KEYS)
        at = head * CORES + jnp.where(odd, 0, 1)
        out = dot_first(prob_ref[at], chosen(odd, (both(odd, v2m, v2o, head) + both(odd, vm, near, head, AT_VALUES))))
        dq = dot_first(dscore_ref[at], chosen(odd, keys))
        for j in range(GROUP):
            piece = slice(j * rows, (j + 1) * rows)
            sent[:, span(head * GROUP + j)] = out[piece].astype(jnp.bfloat16)
            sent[:, span(AT_GRADIENTS + head * GROUP + j)] = dq[piece].astype(jnp.bfloat16)
        dk = other_sum(odd, dscore_ref, stacked(odd, qm, near, head, 0), head, rows)
        dv = other_sum(odd, prob_ref, stacked(odd, gm, near, head, AT_GRADIENTS), head, rows)
        sent[:, span(AT_KEYS + head)] = dk.astype(jnp.bfloat16)
        sent[:, span(AT_VALUES + head)] = dv.astype(jnp.bfloat16)


def own_kernel(
    rank_ref, prob_ref, dscore_ref, qm, gm, km, vm, near, ka, kb, v2m, v2o, backm,
    outm, dqm, dkm, dvm,
):
    rows = qm.shape[0]
    odd = rank_ref[0] % 2 == 1
    for core in range(CORES):

        @pl.when(rank_ref[0] % 2 == core)
        def _():
            for head in range(CORE_HEADS):
                keys = (ka[:, span(head)], kb[:, span(head)]) + both(odd, km, near, head, AT_KEYS)
                values = both(odd, v2m, v2o, head) + both(odd, vm, near, head, AT_VALUES)
                queries = stacked(odd, qm, near, head, 0)
                gradients = stacked(odd, gm, near, head, AT_GRADIENTS)
                out, dq, dk = local_grads(core, prob_ref, dscore_ref, keys, values, queries, head, rows)
                for j in range(GROUP):
                    at = slice(j * rows, (j + 1) * rows)
                    outm[:, span(head * GROUP + j)] = out[at].astype(jnp.bfloat16)
                    dqm[:, span(head * GROUP + j)] = dq[at]
                dkm[:, span(head)] = dk
                dv = local_sum(core, prob_ref, gradients, head, rows)
                dvm[:, span(head)] = dv + backm[:, span(head)].astype(jnp.float32)


def join_kernel(rank_ref, got, outm, dqm, dvm, backo, out_ref, dq_ref, dv_ref):
    odd = rank_ref[0] % CORES
    wide, narrow = outm.shape[1], dvm.shape[1]
    for core in range(CORES):
        here = slice(core * wide, (core + 1) * wide)
        there = slice((1 - core) * wide, (2 - core) * wide)

        @pl.when(odd == core)
        def _():
            out_ref[:, here] = outm[...]
            out_ref[:, there] = got[:, :wide]
            dq_ref[:, here] = dqm[...]
            dq_ref[:, there] = got[:, wide : 2 * wide].astype(jnp.float32)
            dv_ref[:, core * narrow : (core + 1) * narrow] = dvm[...]
            dv_ref[:, (1 - core) * narrow : (2 - core) * narrow] = backo[...].astype(jnp.float32) + got[
                :, AT_VALUES * HEAD_SIZE :
            ].astype(jnp.float32)


def add_kernel(offset, rank_ref, mine, near, backm, backo, target):
    odd = rank_ref[0] % 2
    width = mine.shape[1]
    offset = offset * HEAD_SIZE
    for core in range(CORES):
        here = slice(core * width, (core + 1) * width)
        there = slice((1 - core) * width, (2 - core) * width)

        @pl.when(odd == core)
        def _():
            target[:, here] = mine[...] + backm[...].astype(jnp.float32)
            target[:, there] = near[:, offset : offset + width].astype(jnp.float32) + backo[...].astype(jnp.float32)


def shape(dims, dtype):
    return jax.ShapeDtypeStruct(dims, dtype)


def run(kernel, name, outputs, index, *operands, far=(), scratch=()):
    small = pl.BlockSpec(memory_space=pltpu.SMEM)
    whole = pl.BlockSpec(memory_space=pltpu.VMEM)
    there = pl.BlockSpec(memory_space=pltpu.HBM)
    return pl.pallas_call(
        kernel,
        in_specs=[small] + [there if i in far else whole for i in range(len(operands))],
        out_specs=[whole] * len(outputs),
        out_shape=outputs,
        scratch_shapes=scratch,
        compiler_params=pltpu.CompilerParams(vmem_limit_bytes=40 * 2**20),
        cost_estimate=pl.CostEstimate(flops=COST.get(name, 0) * 1000000, bytes_accessed=1000, transcendentals=0),
        name=name,
    )(index, *operands)


def on_device(queries, keys, values, output_gradient, doc_lengths):
    rows = queries.shape[0]
    devices = lax.axis_size(AXES)
    index = lax.axis_index(AXES).reshape(1)
    docs = doc_lengths.shape[0]

    ahead = [(r, (r + 2) % devices) for r in range(devices)]
    across = [(r, ((r + 2) % devices) ^ 1) for r in range(devices)]
    behind = [(there, here) for here, there in ahead]
    recross = [(there, here) for here, there in across]
    swap = [(r, r ^ 1) for r in range(devices)]

    def moved(value, pairs):
        return lax.ppermute(value, AXES, pairs)

    narrow = shape((rows, keys.shape[1] // CORES), jnp.bfloat16)
    wide = shape((rows, queries.shape[1] // CORES), jnp.bfloat16)
    narrow_sum = shape(narrow.shape, jnp.float32)
    wide_sum = shape(wide.shape, jnp.float32)
    pairs = shape((KEY_VALUE_HEADS, 3 * rows, GROUP * rows), jnp.bfloat16)

    full = shape(keys.shape, jnp.float32)
    all_sent = shape((rows, ALL_SENT * HEAD_SIZE), jnp.bfloat16)
    def copies(count):
        return [pltpu.SemaphoreType.DMA((count,))]

    km, kx = run(split_kernel, "split_keys", [narrow] * 2, index, keys, far=(0,), scratch=copies(2))
    k2m, k2o = moved(km, ahead), moved(kx, across)
    queries, kx = lax.optimization_barrier((queries, kx))
    qm, gm, vm, vx, sent, bias = run(
        rows_kernel, "split_rows",
        [wide, wide, narrow, narrow, all_sent, shape((CORES, 3 * rows, rows), jnp.float32)],
        index, doc_lengths.reshape(1, docs), queries, output_gradient, keys, values,
        far=(1, 2, 3, 4), scratch=copies(8),
    )
    v2m, v2o = moved(vm, ahead), moved(vx, across)
    near = moved(sent, swap)
    (mark,) = run(mark_kernel, "mark", [shape((16, HEAD_SIZE), jnp.bfloat16)], index, k2m)
    ka, kb = run(order_kernel, "far_keys", [narrow] * 2, index, k2m, k2o, mark)
    prob, dvm, dvo = run(
        value_kernel, "value_grads", [pairs, narrow, narrow],
        index, bias, qm, gm, km, near, ka, kb,
    )
    later_rows, dvm, dvo = lax.optimization_barrier((gm, dvm, dvo))
    (near_dprob,) = run(
        near_kernel, "near_values", [shape((KEY_VALUE_HEADS, 2 * rows, GROUP * rows), jnp.float32)],
        index, later_rows, vm, near,
    )
    dvm, dvo, v2o, near_dprob = lax.optimization_barrier((dvm, dvo, v2o, near_dprob))
    dv_back = moved(dvm, behind), moved(dvo, recross)
    dscore, dkm, dko = run(
        key_kernel, "key_grads", [pairs, narrow, narrow],
        index, near_dprob, prob, qm, gm, vm, near, v2m, v2o,
    )
    dk_back = moved(dkm, behind), moved(dko, recross)
    prob, dv_back1 = lax.optimization_barrier((prob, dv_back[1]))
    dv_back = (dv_back[0], dv_back1)
    (sent,) = run(
        sent_kernel, "sent_grads", [all_sent],
        index, prob, dscore, qm, gm, km, vm, near, ka, kb, v2m, v2o,
    )
    got = moved(sent, swap)
    outm, dqm, dkm, dvm = run(
        own_kernel, "own_grads", [wide, wide_sum, narrow_sum, narrow_sum],
        index, prob, dscore, qm, gm, km, vm, near, ka, kb, v2m, v2o, dv_back[0],
    )
    got, dvm = lax.optimization_barrier((got, dvm))
    attended, dq, dv = run(
        join_kernel, "join_rows",
        [shape(queries.shape, jnp.bfloat16), shape(queries.shape, jnp.float32), full],
        index, got, outm, dqm, dvm, dv_back[1],
    )
    (dk,) = run(functools.partial(add_kernel, AT_KEYS), "join_keys", [full], index, dkm, got, *dk_back)
    return attended, dq, dk, dv


def solution(mesh):
    split = P(AXES, None)
    return jax.shard_map(
        on_device,
        mesh=mesh,
        in_specs=(split, split, split, split, P()),
        out_specs=(split, split, split, split),
        check_vma=False,
    )
```
